256 devices in a mesh: sp: 4 (over z_hi, core), fsdp: 64 (over z_lo, y, x).
Axes of the slice: x: 4, y: 4, z: 8 (z_hi: 2, z_lo: 4; z = z_hi * 4 + z_lo), core: 2. Of those that a mesh axis runs over, the one named last changes fastest.
Arguments:
- hidden: bfloat16 [64, 1536, 1536], P('fsdp', 'sp'), may hold values from -16 to 16
- modulation: float32 [64, 2, 1536], P('fsdp'), may hold values from -3 to 3
- cotangent: bfloat16 [64, 1536, 1536], P('fsdp', 'sp'), may hold values from -6 to 6
- frozen_projection: bfloat16 [1536, 4608], P(None, 'fsdp'), may hold values from -0.15625 to 0.15625
- adapter_down_weight: bfloat16 [1536, 64], P('fsdp'), may hold values from -0.15625 to 0.15625
- adapter_up_weight: bfloat16 [64, 4608], P('fsdp'), may hold values from -0.75 to 0.75
- query_key_norm_gains: float32 [2, 128], replicated, may hold values from 0.5 to 2
- windows: int32 [12], replicated, may hold values from 1 to 3, as said below
Outputs:
- attn_out: bfloat16 [64, 1536, 1536], P('fsdp', 'sp')
- grad_down: float32 [1536, 64], P('fsdp')
- grad_up: float32 [64, 4608], P('fsdp')
The draws below stay inside these ranges and needn't reach their ends.
Inputs may be any that keep to these rules, and one draw needn't show every extreme that they name: `windows`: every window is 1 or 3; in every draw some head has 1 and some head has 3.
All inputs are finite; a program needn't handle non-finite values.
Results may differ from the reference program's by a relative error of at most 0.015.
Values may be sent and summed in bfloat16 or wider, within the bound.
No kernel may reach another device: no remote copies, remote signals or barrier semaphores. Data moves between devices by JAX's collectives and lax.ppermute only.
A program may use at most 128 MiB of HBM per device.

```python
import math
import jax
import jax.numpy as jnp
from jax import lax

TOKEN_FEATURES = 1536
HEADS = 12
HEAD_DIM = 128
ADAPTER_RANK = 64
TILE = 384
TILES_DEV = 1
WIDTH = 1536
PROJECTION_WIDTH = 4608
SEQ = 1536
VIDEOS = 64


def draw_windows(key, part):
    key = jax.random.fold_in(key, 11)
    choose_key, ranking_key = jax.random.split(key)
    chosen = jax.random.randint(choose_key, (HEADS,), 0, 2)
    ranking = jax.random.permutation(ranking_key, HEADS)
    chosen = chosen.at[ranking[0]].set(1)
    chosen = chosen.at[ranking[1]].set(0)
    return (1 + 2 * chosen).astype(jnp.int32)


def raised(array, own_key, source, target, blocks, factor):
    def block_of(dim):
        return (jnp.arange(array.shape[dim]) // (array.shape[dim] // blocks)).reshape((-1,) + (1,) * (array.ndim - 1 - dim))

    one_side = jax.random.permutation(own_key, blocks)[block_of(target)]
    far = (block_of(target) + blocks // 2) % blocks
    return jnp.where((block_of(source) == one_side) | (block_of(source) == far), factor * array, array)


def levels(key, dims, cuts, low, high):
    gain, own = 1.0, jax.random.fold_in(key, 6)
    for axis_at, blocks in cuts:
        draws = jnp.exp(jax.random.uniform(jax.random.fold_in(own, axis_at), (blocks,), jnp.float32, low / len(cuts), high / len(cuts)))
        gain = gain * jnp.repeat(draws, dims[axis_at] // blocks).reshape([-1 if axis == axis_at else 1 for axis in range(len(dims))])
    return gain


def scatter_about(stream_key, shape, spread, limit, cuts=(), held_as=jnp.bfloat16):
    drawn = spread * jax.random.normal(stream_key, shape, jnp.float32)
    if cuts:
        drawn = drawn * levels(stream_key, shape, cuts, -0.22, 0.18)
    return jnp.clip(drawn, -limit, limit).astype(held_as)


def bell_draw_with(own_key, shape, scale, most, shards, heavy, kind=jnp.bfloat16):
    values = scale * jax.random.normal(own_key, shape, jnp.float32)
    if shards:
        values = values * levels(own_key, shape, shards, -0.22, 0.18)
    return jnp.clip(raised(values, jax.random.fold_in(own_key, 3), *heavy), -most, most).astype(kind)


def setup_inputs(seed: int = 0) -> dict:
    splits = jax.random.split(jax.random.key(seed), 9)
    return {
        "hidden": bell_draw_with(splits[0], (VIDEOS, SEQ, TOKEN_FEATURES), 1.0, 16.0, ((0, 64), (1, 4)), (0, 2, 64, 4.0)),
        "modulation": scatter_about(splits[1], (VIDEOS, 2, TOKEN_FEATURES), 0.5, 3.0, ((0, 64),), jnp.float32),
        "cotangent": scatter_about(splits[2], (VIDEOS, SEQ, WIDTH), 1.0, 6.0, ((0, 64), (1, 4))),
        "frozen_projection": scatter_about(splits[3], (TOKEN_FEATURES, PROJECTION_WIDTH), TOKEN_FEATURES ** -0.5, 0.15625, ((1, 64),)),
        "adapter_down_weight": scatter_about(splits[4], (TOKEN_FEATURES, ADAPTER_RANK), TOKEN_FEATURES ** -0.5, 0.15625, ((0, 64),)),
        "adapter_up_weight": scatter_about(splits[5], (ADAPTER_RANK, PROJECTION_WIDTH), ADAPTER_RANK ** -0.5, 0.75, ((0, 64),)),
        "query_key_norm_gains": jnp.clip(jnp.exp(jax.random.uniform(splits[6], (2, HEAD_DIM), jnp.float32, math.log(0.5), math.log(2.0))), 0.5, 2.0),
        "windows": draw_windows(jax.random.fold_in(splits[8], 71), 0),
    }


EPSILON = 1e-06
MASKED = -1e+30

def modulated_norm(hidden_token_rows, modulation):
    values_wide = hidden_token_rows.astype(jnp.float32)
    average = lax.optimization_barrier(jnp.mean(values_wide, axis=-1, keepdims=True))
    centred = values_wide - average
    variance = lax.optimization_barrier(jnp.mean(centred * centred, axis=-1, keepdims=True))
    unit_rows = centred * lax.rsqrt(variance + EPSILON)
    return (unit_rows * (1.0 + modulation[0]) + modulation[1]).astype(jnp.bfloat16)

def head_norm(raw_vals):
    inverse = lax.rsqrt(lax.optimization_barrier(jnp.mean(raw_vals * raw_vals, axis=-1, keepdims=True)) + EPSILON)
    return (raw_vals * inverse, inverse)

def head_norm_grad(unit_vals, inverse, gain_row, incoming_gradient):
    scaled = incoming_gradient * gain_row
    return inverse * (scaled - unit_vals * lax.optimization_barrier(jnp.mean(unit_vals * scaled, axis=-1, keepdims=True)))

def window_mask(tile_count, tile_len, radius, first_tile, total_tiles):
    tile_ids = first_tile + jnp.arange(tile_count, dtype=jnp.int32)
    offsets = jnp.arange(3, dtype=jnp.int32) - 1
    target = tile_ids[:, None] + offsets[None, :]
    allowed = (jnp.abs(offsets)[None, :] <= radius) & (target >= 0) & (target < total_tiles)
    return jnp.repeat(allowed, tile_len, axis=1)

def attend_head(query, keys_ext, values_ext, incoming_gradient, radius, first_tile, total_tiles):
    tile_count, tile_len, depth = query.shape
    keys_near = jnp.concatenate([keys_ext[offset:offset + tile_count] for offset in range(3)], axis=1)
    values_near = jnp.concatenate([values_ext[offset:offset + tile_count] for offset in range(3)], axis=1)
    allowed = window_mask(tile_count, tile_len, radius, first_tile, total_tiles)
    factor = depth ** (-0.5)
    query_wide = query.astype(jnp.float32)
    keys_wide = keys_near.astype(jnp.float32)
    values_wide = values_near.astype(jnp.float32)
    scores = jnp.einsum('nqd,nkd->nqk', query_wide, keys_wide) * factor
    scores = jnp.where(allowed[:, None, :], scores, MASKED)
    exp_scores = jnp.exp(scores - lax.optimization_barrier(jnp.max(scores, axis=-1, keepdims=True)))
    attn_probs = exp_scores / lax.optimization_barrier(jnp.sum(exp_scores, axis=-1, keepdims=True))
    rounded_probs = attn_probs.astype(jnp.bfloat16)
    step_output = jnp.einsum('nqk,nkd->nqd', rounded_probs.astype(jnp.float32), values_wide).astype(jnp.bfloat16)
    upstream_wide = incoming_gradient.astype(jnp.float32)
    grad_probs = jnp.einsum('nqd,nkd->nqk', upstream_wide, values_wide)
    row_delta = lax.optimization_barrier(jnp.sum(upstream_wide * step_output.astype(jnp.float32), axis=-1, keepdims=True))
    grad_scores = (attn_probs * (grad_probs - row_delta) * factor).astype(jnp.bfloat16)
    scores_wide = grad_scores.astype(jnp.float32)
    grad_query = jnp.einsum('nqk,nkd->nqd', scores_wide, keys_wide)
    grad_keys = jnp.einsum('nqk,nqd->nkd', scores_wide, query_wide).reshape(tile_count, 3, tile_len, depth)
    grad_values = jnp.einsum('nqk,nqd->nkd', rounded_probs.astype(jnp.float32), upstream_wide).reshape(tile_count, 3, tile_len, depth)
    return (step_output, grad_query, grad_keys, grad_values)

def split_heads(values_flat, tile_count):
    return jnp.moveaxis(values_flat.reshape(tile_count, TILE, HEADS, HEAD_DIM), 2, 0)

def merge_heads(per_head):
    heads_n, tile_count, tile_len, depth = per_head.shape
    return jnp.moveaxis(per_head, 0, 2).reshape(tile_count * tile_len, heads_n * depth)

def rounded(values_wide):
    return lax.optimization_barrier(values_wide.astype(jnp.bfloat16)).astype(jnp.float32)

def collect_parts(parts, tile_total):
    own_part = parts[:, :, 1]
    zero_tile = jnp.zeros_like(own_part[:, :1])
    from_right = jnp.concatenate([parts[:, 1:, 0], zero_tile], axis=1)
    from_left = jnp.concatenate([zero_tile, parts[:, :-1, 2]], axis=1)
    tile_ids = jnp.arange(tile_total, dtype=jnp.int32)
    right_cross = ((tile_ids + 1) % TILES_DEV == 0)[None, :, None, None]
    left_cross = (tile_ids % TILES_DEV == 0)[None, :, None, None]
    right_term = jnp.where(right_cross, rounded(from_right), from_right)
    left_term = jnp.where(left_cross, rounded(from_left), from_left)
    return own_part + right_term + left_term

def single_video_input(hidden_token_rows, modulation, incoming_gradient, frozen_projection, adapter_down_weight, adapter_up_weight, query_key_norm_gains, window_radius_list):
    normalized_rows = modulated_norm(hidden_token_rows, modulation)
    reduced_rank_rows = jnp.dot(normalized_rows, adapter_down_weight, preferred_element_type=jnp.float32).astype(jnp.bfloat16)
    blended_projection = jnp.dot(normalized_rows, frozen_projection, preferred_element_type=jnp.float32) + jnp.dot(reduced_rank_rows, adapter_up_weight, preferred_element_type=jnp.float32)
    width = HEADS * HEAD_DIM
    seq_len = hidden_token_rows.shape[0]
    tile_total = seq_len // TILE
    query_unit, query_inverse = head_norm(blended_projection[:, :width].reshape(seq_len, HEADS, HEAD_DIM))
    key_unit, key_inverse = head_norm(blended_projection[:, width:2 * width].reshape(seq_len, HEADS, HEAD_DIM))
    queries = (query_unit * query_key_norm_gains[0]).astype(jnp.bfloat16).reshape(seq_len, width)
    keys = (key_unit * query_key_norm_gains[1]).astype(jnp.bfloat16).reshape(seq_len, width)
    values = blended_projection[:, 2 * width:].astype(jnp.bfloat16)
    padding = ((0, 0), (1, 1), (0, 0), (0, 0))
    keys_ext = jnp.pad(split_heads(keys, tile_total), padding)
    values_ext = jnp.pad(split_heads(values, tile_total), padding)

    def per_head(entry_list):
        return attend_head(entry_list[0], entry_list[1], entry_list[2], entry_list[3], entry_list[4], 0, tile_total)
    outputs, grad_query, key_parts, value_parts = lax.map(per_head, (split_heads(queries, tile_total), keys_ext, values_ext, split_heads(incoming_gradient, tile_total), window_radius_list))
    grad_keys = merge_heads(collect_parts(key_parts, tile_total)).reshape(seq_len, HEADS, HEAD_DIM)
    grad_values = merge_heads(collect_parts(value_parts, tile_total))
    query_raw = head_norm_grad(query_unit, query_inverse, query_key_norm_gains[0], merge_heads(grad_query).reshape(seq_len, HEADS, HEAD_DIM))
    key_raw = head_norm_grad(key_unit, key_inverse, query_key_norm_gains[1], grad_keys)
    gradient_blended = jnp.concatenate([query_raw.reshape(seq_len, width), key_raw.reshape(seq_len, width), grad_values], axis=1).astype(jnp.bfloat16)
    up_weight_share = jnp.dot(reduced_rank_rows.T, gradient_blended, preferred_element_type=jnp.float32)
    reduced_rank_gradient = jnp.dot(gradient_blended, adapter_up_weight.T, preferred_element_type=jnp.float32).astype(jnp.bfloat16)
    down_weight_share = jnp.dot(normalized_rows.T, reduced_rank_gradient, preferred_element_type=jnp.float32)
    return (merge_heads(outputs), down_weight_share, up_weight_share)

def reference(hidden, modulation, cotangent, frozen_projection, adapter_down_weight, adapter_up_weight, query_key_norm_gains, windows):
    window_radius_list = (windows - 1) // 2

    def step_video(totals, entry_list):
        step_output, down_weight_share, up_weight_share = single_video_input(entry_list[0], entry_list[1], entry_list[2], frozen_projection, adapter_down_weight, adapter_up_weight, query_key_norm_gains, window_radius_list)
        return ((totals[0] + down_weight_share, totals[1] + up_weight_share), step_output)
    start_totals = (jnp.zeros((TOKEN_FEATURES, ADAPTER_RANK), jnp.float32), jnp.zeros((ADAPTER_RANK, 3 * HEADS * HEAD_DIM), jnp.float32))
    totals, attn_out = lax.scan(step_video, start_totals, (hidden, modulation, cotangent))
    return (attn_out, totals[0], totals[1])
```

```python
import functools
import math

import jax
import jax.numpy as jnp
from jax import lax
from jax.experimental import pallas as pl
from jax.experimental.pallas import tpu as pltpu
from jax.sharding import Mesh, PartitionSpec as P

HEADS = 12
HALF = 6
DIM = 128
TILE = 384
FEATURES = 1536
RANK = 64
COLS = 72
EPSILON = 1e-06
SCALE = DIM**-0.5
LOG2E = math.log2(math.e)
AXES = ("zh", "c", "zl", "y", "x")
FSDP = ("zl", "y", "x")
NT = (((1,), (1,)), ((), ()))
F32 = jnp.float32
BF16 = jnp.bfloat16


def rows_dot(a, b):
    return lax.dot_general(a, b, NT, preferred_element_type=F32)


def dot(a, b):
    return jnp.dot(a, b, preferred_element_type=F32)


def norm_kernel(hidden, modulation, out):
    wide = hidden[...].astype(F32)
    centred = wide - jnp.mean(wide, axis=-1, keepdims=True)
    variance = jnp.mean(centred * centred, axis=-1, keepdims=True)
    unit = centred * lax.rsqrt(variance + EPSILON)
    out[...] = (unit * (1.0 + modulation[0:1, :]) + modulation[1:2, :]).astype(BF16)


def modulated_norm(hidden, modulation):
    rows = 128
    return pl.pallas_call(
        norm_kernel,
        grid=(TILE // rows,),
        in_specs=[
            pl.BlockSpec((rows, FEATURES), lambda i: (i, 0)),
            pl.BlockSpec((2, FEATURES), lambda i: (0, 0)),
        ],
        out_specs=pl.BlockSpec((rows, FEATURES), lambda i: (i, 0)),
        out_shape=jax.ShapeDtypeStruct((TILE, FEATURES), BF16),
        compiler_params=pltpu.CompilerParams(vmem_limit_bytes=32 << 20),
        name="modulated_norm",
    )(hidden, modulation)


def project_kernel(
    table, own, other, near, far, wa, wb, down_t, down, up, gains, qkv, inverse, low_t, x, low
):
    n = pl.program_id(0)

    @pl.when(n == 0)
    def _():
        own_at = pl.multiple_of(table[6], TILE)
        half = TILE // 2
        near_at = pl.multiple_of(2 * TILE + table[7] * half, half)
        far_at = pl.multiple_of(2 * TILE + (1 - table[7]) * half, half)
        x[pl.ds(own_at, TILE), :] = own[...]
        x[pl.ds(pl.multiple_of(TILE - table[6], TILE), TILE), :] = other[...]
        x[pl.ds(near_at, half), :] = near[...]
        x[pl.ds(far_at, half), :] = far[...]
        inverse[...] = jnp.zeros_like(inverse)
        for m in range(3):
            rows = slice(m * TILE, (m + 1) * TILE)
            low[rows, :] = dot(x[rows, :], down[...]).astype(BF16)
            low_t[:, rows] = rows_dot(down_t[...], x[rows, :]).astype(BF16)

    half_k = FEATURES // 2
    lane = lax.broadcasted_iota(jnp.int32, (TILE, DIM), 1)
    gain = jnp.where(n < 2, gains[0:1, :], gains[1:2, :])
    for m in range(3):
        rows = slice(m * TILE, (m + 1) * TILE)
        raw = (
            rows_dot(x[rows, :half_k], wa[...])
            + rows_dot(x[rows, half_k:], wb[...])
            + dot(low[rows, :], up[...])
        )

        @pl.when(n < 4)
        def _():
            kept = inverse[rows, :]
            for i in range(3):
                part = raw[:, i * DIM : (i + 1) * DIM]
                inv = lax.rsqrt(jnp.mean(part * part, axis=-1, keepdims=True) + EPSILON)
                qkv[rows, i * DIM : (i + 1) * DIM] = (part * inv * gain).astype(BF16)
                kept = jnp.where(lane == n * 3 + i, inv, kept)
            inverse[rows, :] = kept

        @pl.when(n >= 4)
        def _():
            qkv[rows, :] = raw.astype(BF16)


def project(table, own, other, near, far, wa, wb, down, up, gains):
    tokens = 3 * TILE
    whole = lambda *shape: pl.BlockSpec(shape, lambda n, t: (0,) * len(shape))
    return pl.pallas_call(
        project_kernel,
        grid_spec=pltpu.PrefetchScalarGridSpec(
            num_scalar_prefetch=1,
            grid=(6,),
            in_specs=[
                whole(TILE, FEATURES),
                whole(TILE, FEATURES),
                whole(TILE // 2, FEATURES),
                whole(TILE // 2, FEATURES),
                pl.BlockSpec((TILE, FEATURES // 2), lambda n, t: (t[n], 0)),
                pl.BlockSpec((TILE, FEATURES // 2), lambda n, t: (t[n], 0)),
                whole(RANK, FEATURES),
                whole(FEATURES, RANK),
                pl.BlockSpec((RANK, TILE), lambda n, t: (0, n)),
                whole(2, DIM),
            ],
            out_specs=[
                pl.BlockSpec((tokens, TILE), lambda n, t: (0, n)),
                whole(tokens, DIM),
                whole(RANK, tokens),
            ],
            scratch_shapes=[
                pltpu.VMEM((tokens, FEATURES), BF16),
                pltpu.VMEM((tokens, RANK), BF16),
            ],
        ),
        out_shape=[
            jax.ShapeDtypeStruct((tokens, 6 * TILE), BF16),
            jax.ShapeDtypeStruct((tokens, DIM), F32),
            jax.ShapeDtypeStruct((RANK, tokens), BF16),
        ],
        compiler_params=pltpu.CompilerParams(vmem_limit_bytes=56 << 20),
        cost_estimate=pl.CostEstimate(
            flops=2 * tokens * FEATURES * 6 * TILE, bytes_accessed=20 << 20, transcendentals=0
        ),
        name="project",
    )(table, own, other, near, far, wa, wb, down.T, down, up, gains)


def column_of(inverse, at, rows):
    lane = lax.broadcasted_iota(jnp.int32, (rows, DIM), 1)
    return jnp.sum(jnp.where(lane == at, inverse, 0.0), axis=-1, keepdims=True)


def norm_grad(grad, rounded, gain, inv):
    held = rounded.astype(F32)
    along = jnp.mean(held * grad, axis=-1, keepdims=True)
    return inv * (gain * grad - (held / gain) * along)


def attend(query, cot, cot_t, key, value, key_t, value_t):
    exps = jnp.exp2(rows_dot(key, query) * (SCALE * LOG2E))
    inv_sum = 1.0 / jnp.sum(exps, axis=0, keepdims=True)
    probs = exps * inv_sum
    rounded = probs.astype(BF16)
    out_t = dot(value_t, rounded).astype(BF16).astype(F32)
    delta = jnp.sum(cot_t * out_t, axis=0, keepdims=True)
    grad_probs = rows_dot(value, cot)
    grad_scores = (probs * (grad_probs - delta) * SCALE).astype(BF16)
    grad_query = dot(key_t, grad_scores).T
    return out_t.T.astype(BF16), inv_sum, delta, rounded, grad_scores, grad_query


def boundary_kernel(wide, q, k, v, cot, inverse, gains, out, stats, grad_q, grad_k, grad_v):
    h = pl.program_id(0)
    own = slice(TILE, 2 * TILE)
    query, cot_in = q[own, :], cot[...]
    cot_t = cot_in.astype(F32).T
    inv = column_of(inverse[own, :], h, TILE)

    def run(lo, hi):
        key, value = k[lo:hi, :], v[lo:hi, :]
        key_t = key.astype(F32).T.astype(BF16)
        value_t = value.astype(F32).T.astype(BF16)
        o, inv_sum, delta, rounded, grad_scores, grad_query = attend(
            query, cot_in, cot_t, key, value, key_t, value_t
        )
        out[...] = o
        stats[0, 0:1, :] = inv_sum
        stats[0, 1:2, :] = delta
        grad_q[...] = norm_grad(grad_query, query, gains[0:1, :], inv).astype(BF16)
        last = min(hi, 2 * TILE) - lo
        grad_k[lo : lo + last, :] = dot(grad_scores[:last], query)
        grad_v[lo : lo + last, :] = dot(rounded[:last], cot_in)

    @pl.when(wide[h] > 0)
    def _():
        run(0, 3 * TILE)

    @pl.when(wide[h] == 0)
    def _():
        grad_k[:TILE, :] = jnp.zeros((TILE, DIM), F32)
        grad_v[:TILE, :] = jnp.zeros((TILE, DIM), F32)
        run(TILE, 2 * TILE)


def outer_kernel(
    wide, q, k, v, cot, inverse, gains, part_k, part_v, out, grad_q, grad_k, grad_v
):
    h = pl.program_id(0)
    query, cot_in = q[...], cot[...]
    cot_t = cot_in.astype(F32).T
    inv = column_of(inverse[...], h, TILE)

    def run(hi):
        key, value = k[:hi, :], v[:hi, :]
        key_t = key.astype(F32).T.astype(BF16)
        value_t = value.astype(F32).T.astype(BF16)
        o, _, _, rounded, grad_scores, grad_query = attend(
            query, cot_in, cot_t, key, value, key_t, value_t
        )
        out[...] = o
        grad_q[...] = norm_grad(grad_query, query, gains[0:1, :], inv).astype(BF16)
        grad_k[:hi, :] = part_k[:hi, :] + dot(grad_scores, query)
        grad_v[:hi, :] = part_v[:hi, :] + dot(rounded, cot_in)

    @pl.when(wide[h] > 0)
    def _():
        run(2 * TILE)

    @pl.when(wide[h] == 0)
    def _():
        run(TILE)
        grad_k[TILE:, :] = part_k[TILE:, :]
        grad_v[TILE:, :] = part_v[TILE:, :]


def finish_kernel(
    table, q, k, v, cot, stats, inverse, gains, part_k, part_v, grad_qo, grad_qb,
    low_t, up_q, up_k, up_v, own, other,
    out_q, out_k, out_v, out_down, sum_k, sum_v, rank_t,
):
    h = pl.program_id(0)

    @pl.when(h == 0)
    def _():
        rank_t[...] = jnp.zeros_like(rank_t)

    sum_k[...] = part_k[...]
    sum_v[...] = part_v[...]

    @pl.when(table[8 + h] > 0)
    def _():
        query, cot_in = q[...], cot[...]
        key, value = k[TILE:, :], v[TILE:, :]
        probs = jnp.exp2(rows_dot(key, query) * (SCALE * LOG2E)) * stats[0, 0:1, :]
        grad_probs = rows_dot(value, cot_in)
        grad_scores = (probs * (grad_probs - stats[0, 1:2, :]) * SCALE).astype(BF16)
        sum_k[TILE:, :] += dot(grad_scores, query)
        sum_v[TILE:, :] += dot(probs.astype(BF16), cot_in)

    inv = column_of(inverse[...], HALF + h, 2 * TILE)
    grad_k = norm_grad(sum_k[...], k[...], gains[1:2, :], inv).astype(BF16)
    grad_v = sum_v[...].astype(BF16)
    left = low_t[...]
    out_q[...] = (dot(left[:, :TILE], grad_qo[...]) + dot(left[:, TILE:], grad_qb[...])).astype(BF16)
    out_k[...] = dot(left, grad_k).astype(BF16)
    out_v[...] = dot(left, grad_v).astype(BF16)
    rank_t[:, :TILE] += rows_dot(up_q[...], grad_qo[...])
    rank_t[:, TILE:] += rows_dot(up_q[...], grad_qb[...])
    rank_t[...] += rows_dot(up_k[...], grad_k) + rows_dot(up_v[...], grad_v)

    @pl.when(h == HALF - 1)
    def _():
        outer = rank_t[:, :TILE].astype(BF16)
        inner = rank_t[:, TILE:].astype(BF16)
        first = table[6] == 0
        mine = jnp.where(first, outer, inner)
        others = jnp.where(first, inner, outer)
        out_down[...] = (dot(mine, own[...]) + dot(others, other[...])).astype(BF16)


SMEM = pl.BlockSpec(memory_space=pltpu.SMEM)


def per_head(rows, at=0, block=0):
    return pl.BlockSpec((rows, DIM), lambda h: (block, at + h))


def constant(*shape):
    return pl.BlockSpec(shape, lambda h: (0,) * len(shape))


def attention_cost(pairs):
    return pl.CostEstimate(
        flops=12 * TILE * TILE * DIM * HALF * pairs,
        bytes_accessed=8 << 20,
        transcendentals=TILE * TILE * HALF * pairs,
    )


def shaped(*shape, dtype=BF16):
    return jax.ShapeDtypeStruct(shape, dtype)


PARAMS = pltpu.CompilerParams(vmem_limit_bytes=48 << 20)


def boundary(wide, qkv, cot, inverse, gains):
    width = HALF * DIM
    return pl.pallas_call(
        boundary_kernel,
        grid=(HALF,),
        in_specs=[
            SMEM,
            per_head(3 * TILE),
            per_head(3 * TILE, HALF),
            per_head(3 * TILE, 2 * HALF),
            per_head(TILE),
            constant(3 * TILE, DIM),
            constant(2, DIM),
        ],
        out_specs=[
            per_head(TILE),
            pl.BlockSpec((1, 2, TILE), lambda h: (h, 0, 0)),
            per_head(TILE),
            per_head(2 * TILE),
            per_head(2 * TILE),
        ],
        out_shape=[
            shaped(TILE, width),
            shaped(HALF, 2, TILE, dtype=F32),
            shaped(TILE, width),
            shaped(2 * TILE, width, dtype=F32),
            shaped(2 * TILE, width, dtype=F32),
        ],
        compiler_params=PARAMS,
        cost_estimate=attention_cost(3),
        name="boundary",
    )(wide, qkv, qkv, qkv, cot, inverse, gains)


def outer(wide, qkv, cot, inverse, gains, part_k, part_v):
    width = HALF * DIM
    return pl.pallas_call(
        outer_kernel,
        grid=(HALF,),
        in_specs=[
            SMEM,
            per_head(TILE),
            per_head(2 * TILE, HALF),
            per_head(2 * TILE, 2 * HALF),
            per_head(TILE),
            constant(TILE, DIM),
            constant(2, DIM),
            per_head(2 * TILE),
            per_head(2 * TILE),
        ],
        out_specs=[per_head(TILE), per_head(TILE), per_head(2 * TILE), per_head(2 * TILE)],
        out_shape=[
            shaped(TILE, width),
            shaped(TILE, width),
            shaped(2 * TILE, width, dtype=F32),
            shaped(2 * TILE, width, dtype=F32),
        ],
        compiler_params=PARAMS,
        cost_estimate=attention_cost(2),
        name="outer",
    )(wide, qkv, qkv, qkv, cot, inverse, gains, part_k, part_v)


def finish(
    table, qkv, cot, stats, inverse, gains, part_k, part_v, grad_qo, grad_qb, low_t, up, own, other
):
    width = HALF * DIM
    up_at = lambda at: pl.BlockSpec((RANK, DIM), lambda h: (0, at + h))
    return pl.pallas_call(
        finish_kernel,
        grid=(HALF,),
        in_specs=[
            SMEM,
            per_head(TILE, 0, 2),
            per_head(2 * TILE, HALF),
            per_head(2 * TILE, 2 * HALF),
            per_head(TILE),
            pl.BlockSpec((1, 2, TILE), lambda h: (h, 0, 0)),
            constant(2 * TILE, DIM),
            constant(2, DIM),
            per_head(2 * TILE),
            per_head(2 * TILE),
            per_head(TILE),
            per_head(TILE),
            constant(RANK, 2 * TILE),
            up_at(0),
            up_at(HALF),
            up_at(2 * HALF),
            constant(TILE, FEATURES),
            constant(TILE, FEATURES),
        ],
        out_specs=[up_at(0), up_at(0), up_at(0), constant(RANK, FEATURES)],
        out_shape=[
            shaped(RANK, width),
            shaped(RANK, width),
            shaped(RANK, width),
            shaped(RANK, FEATURES),
        ],
        scratch_shapes=[
            pltpu.VMEM((2 * TILE, DIM), F32),
            pltpu.VMEM((2 * TILE, DIM), F32),
            pltpu.VMEM((RANK, 2 * TILE), F32),
        ],
        compiler_params=PARAMS,
        cost_estimate=attention_cost(1),
        name="finish",
    )(
        table, qkv, qkv, qkv, cot, stats, inverse, gains, part_k, part_v, grad_qo, grad_qb,
        low_t, up, up, up, own, other,
    )


def swap(block, axis):
    return lax.ppermute(block, axis, [(0, 1), (1, 0)])


def hop(block, axis, count, step):
    return lax.ppermute(block, axis, [(i, (i + step) % count) for i in range(count)])


def ring_gather(block, axis):
    me = lax.axis_index(axis)
    half = block.shape[0] // 2
    low, high = block[:half], block[half:]
    below_low, above_high = hop(low, axis, 4, 1), hop(high, axis, 4, -1)
    below_high, above_low = hop(high, axis, 4, 1), hop(low, axis, 4, -1)
    far_low, far_high = hop(below_low, axis, 4, 1), hop(above_high, axis, 4, -1)
    out = jnp.zeros((4,) + block.shape, block.dtype)
    out = lax.dynamic_update_index_in_dim(out, block, me, 0)
    for distance, pair in ((3, (below_low, below_high)), (1, (above_low, above_high)), (2, (far_low, far_high))):
        at = lax.rem(me + distance, 4)
        start = (at,) + (0,) * block.ndim
        out = lax.dynamic_update_slice(out, pair[0][None], start)
        start = (at, half) + (0,) * (block.ndim - 1)
        out = lax.dynamic_update_slice(out, pair[1][None], start)
    return out


def pick(options, at):
    out = options[0]
    for i in range(1, len(options)):
        out = jnp.where(at == i, options[i], out)
    return out


def gather_weights(frozen, down, up):
    core, zl = lax.axis_index("c"), lax.axis_index("zl")
    place = lax.axis_index("y") * 4 + lax.axis_index("x")
    packed = jnp.concatenate(
        [frozen.T, down.reshape(1, FEATURES), up.reshape(3, FEATURES), jnp.zeros((4, FEATURES), BF16)]
    )
    along = ("zh", "zl")
    planes = [packed, hop(packed, along, 8, -1), hop(packed, along, 8, 2), hop(packed, along, 8, 1)]
    third = (place * COLS + lax.broadcasted_iota(jnp.int32, (COLS, 1), 0)) // TILE
    first = jnp.where(core == 0, pick([0, 0, 1], third), pick([1, 2, 0], third))
    second = jnp.where(core == 0, pick([3, 1, 2], third), pick([2, 3, 3], third))
    columns = [plane[:COLS] for plane in planes]
    small = [plane[COLS : COLS + 4] for plane in planes]
    block = jnp.concatenate(
        [pick(columns, (first - zl + 4) % 4), pick(columns, (second - zl + 4) % 4)]
        + [pick(small, (plane - zl + 4) % 4) for plane in range(4)]
    )
    half_k = FEATURES // 2
    a = ring_gather(block[:, :half_k], "x")
    b = ring_gather(block[:, half_k:], "y")
    a = ring_gather(a, "y")
    b = jnp.swapaxes(ring_gather(b, "x"), 0, 1)
    flat = 3 * TILE

    def rows_of(g):
        return jnp.concatenate(
            [g[:, :, :COLS].reshape(flat, half_k), g[:, :, COLS : 2 * COLS].reshape(flat, half_k)]
        )

    rest = jnp.concatenate([a[:, :, 2 * COLS :], b[:, :, 2 * COLS :]], axis=3)
    rest = rest.reshape(16, 4, 4, FEATURES).transpose(1, 0, 2, 3).reshape(64, 4, FEATURES)
    down_full = rest[:, 0].reshape(FEATURES, RANK)
    at = core * HALF * DIM
    up_mine = jnp.concatenate(
        [lax.dynamic_slice(rest[:, 1 + i], (0, at), (RANK, HALF * DIM)) for i in range(3)], axis=1
    )
    return rows_of(a), rows_of(b), down_full, up_mine


def reduce_adapter(out_q, out_k, out_v, out_down):
    core = lax.axis_index("c")
    width = HALF * DIM
    down = out_down.reshape(RANK, 64, FEATURES // 64).transpose(1, 2, 0).reshape(64, FEATURES)
    payload = jnp.concatenate([out_q, out_k, out_v, down], axis=1)
    parts = lax.all_to_all(payload, FSDP, 0, 0, tiled=True)
    mine = jnp.sum(parts.astype(F32), axis=0).reshape(-1, DIM)
    above = swap(mine, "zh")
    across = swap(mine, "c")
    diagonal = lax.ppermute(mine, ("zh", "c"), [(i, 3 - i) for i in range(4)])
    own, other = (mine + above).reshape(-1), (across + diagonal).reshape(-1)
    low, high = jnp.where(core == 0, own, other), jnp.where(core == 0, other, own)
    grad_up = jnp.concatenate(
        [side[i * width : (i + 1) * width] for i in range(3) for side in (low, high)]
    )
    grad_down = (own + other)[3 * width :]
    return grad_down.reshape(FEATURES // 64, RANK), grad_up.reshape(1, -1)


def local(hidden, modulation, cotangent, frozen, down, up, gains, windows):
    high, core = lax.axis_index("zh"), lax.axis_index("c")
    width = HALF * DIM
    outermost = core == high
    wa, wb, down_full, up_mine = gather_weights(frozen, down, up)

    own = modulated_norm(hidden[0], modulation[0])
    other = swap(own, "c")
    edge = jnp.where(outermost, other, own)
    near = swap(lax.dynamic_slice(edge, (core * (TILE // 2), 0), (TILE // 2, FEATURES)), "zh")
    far = swap(near, "c")

    cot_own = lax.dynamic_slice(cotangent[0], (0, core * width), (TILE, width))
    cot_other = swap(lax.dynamic_slice(cotangent[0], (0, (1 - core) * width), (TILE, width)), "c")
    cot_outer = jnp.where(outermost, cot_own, cot_other)
    cot_edge = jnp.where(outermost, cot_other, cot_own)
    cot_halo = swap(cot_edge, "zh")

    wide = (lax.dynamic_slice(windows, (core * HALF,), (HALF,)) > 1).astype(jnp.int32)
    order = jnp.where(core == 0, jnp.array([0, 1, 4, 2, 5, 3]), jnp.array([2, 0, 3, 1, 4, 5]))
    own_at = jnp.where(outermost, 0, TILE)
    table = jnp.concatenate([order, jnp.stack([own_at, core]), wide]).astype(jnp.int32)

    qkv, inverse, low_t = project(table, own, other, near, far, wa, wb, down_full, up_mine, gains)
    out_edge, stats, grad_qb, part_k, part_v = boundary(wide, qkv, cot_edge, inverse, gains)
    stats = swap(stats, "zh")
    out_outer, grad_qo, part_k, part_v = outer(
        wide, qkv, cot_outer, inverse, gains, part_k, part_v
    )
    back = swap(jnp.where(outermost, out_edge, out_outer), "c")
    kept = jnp.where(outermost, out_outer, out_edge)
    attn_out = jnp.concatenate(
        [jnp.where(core == 0, kept, back), jnp.where(core == 0, back, kept)], axis=1
    )
    sums = finish(
        table, qkv, cot_halo, stats, inverse, gains, part_k, part_v, grad_qo, grad_qb,
        low_t, up_mine, own, other,
    )
    grad_down, grad_up = reduce_adapter(*sums)
    return attn_out[None], grad_down, grad_up


def solution(mesh):
    split = Mesh(mesh.devices.reshape(2, 2, 4, 4, 4), AXES)
    sp = ("zh", "c")
    in_specs = (
        P(FSDP, sp, None),
        P(FSDP, None, None),
        P(FSDP, sp, None),
        P(None, FSDP),
        P(FSDP, None),
        P(FSDP, None),
        P(),
        P(),
    )
    out_specs = (P(FSDP, sp, None), P(FSDP, None), P(FSDP, None))
    return jax.shard_map(local, mesh=split, in_specs=in_specs, out_specs=out_specs, check_vma=False)
```

```python
import functools
import math

import jax
import jax.numpy as jnp
from jax import lax
from jax.experimental import pallas as pl
from jax.experimental.pallas import tpu as pltpu
from jax.sharding import Mesh, PartitionSpec as P

HEADS = 12
HALF = 6
DIM = 128
TILE = 384
FEATURES = 1536
RANK = 64
COLS = 72
ROWS = 2 * COLS + 16
KINDS = (0, 1, 2, 2, 0, 1), (1, 2, 0, 0, 1, 2)
GROUP = 3
EPSILON = 1e-06
SCALE = DIM**-0.5
LOG2E = math.log2(math.e)
AXES = ("zh", "c", "zl", "y", "x")
FSDP = ("zl", "y", "x")
NT = (((1,), (1,)), ((), ()))
F32 = jnp.float32
BF16 = jnp.bfloat16


def rows_dot(a, b):
    return lax.dot_general(a, b, NT, preferred_element_type=F32)


def dot(a, b):
    return jnp.dot(a, b, preferred_element_type=F32)


def norm_kernel(hidden, modulation, out):
    wide = hidden[...].astype(F32)
    centred = wide - jnp.mean(wide, axis=-1, keepdims=True)
    variance = jnp.mean(centred * centred, axis=-1, keepdims=True)
    unit = centred * lax.rsqrt(variance + EPSILON)
    out[...] = (unit * (1.0 + modulation[0:1, :]) + modulation[1:2, :]).astype(BF16)


def modulated_norm(hidden, modulation):
    rows = 128
    return pl.pallas_call(
        norm_kernel,
        grid=(TILE // rows,),
        in_specs=[
            pl.BlockSpec((rows, FEATURES), lambda i: (i, 0)),
            pl.BlockSpec((2, FEATURES), lambda i: (0, 0)),
        ],
        out_specs=pl.BlockSpec((rows, FEATURES), lambda i: (i, 0)),
        out_shape=jax.ShapeDtypeStruct((TILE, FEATURES), BF16),
        compiler_params=pltpu.CompilerParams(vmem_limit_bytes=32 << 20),
        name="modulated_norm",
    )(hidden, modulation)


def project_kernel(
    place, xo, xb, xh, *refs,
):
    *pieces, down, up, gains, qkv0, qkv1, inverse, low_t, up0, up1 = refs[:14]
    x, spread, w, low, up_here, sems = refs[14:]
    core, outer = place[0], place[1]
    wide = 2 * TILE
    tiles = [slice(m * TILE, (m + 1) * TILE) for m in range(3)]
    bands = [slice(n * wide, (n + 1) * wide) for n in range(3)]
    copies = [
        pltpu.make_async_copy(tile, x.at[rows, :], sems.at[m])
        for m, (tile, rows) in enumerate(zip((xo, xb, xh), tiles))
    ]
    for distance, j, piece in zip((0, 1, 3, 2, 2), (0, 0, 0, 0, 2), pieces):
        i = lax.rem(outer + distance, 4)
        for k in range(piece.shape[0]):
            slot = jnp.where(core == 0, 4 * i + j + k, 4 * (j + k) + i)
            sem = sems.at[len(copies)]
            copies.append(pltpu.make_async_copy(piece.at[k], spread.at[slot], sem))
    for copy in copies:
        copy.start()
    inverse[...] = jnp.zeros_like(inverse)
    for copy in copies[:3]:
        copy.wait()
    for m, rows in enumerate(tiles):
        part = dot(x[rows, :], down[...])
        low[rows, :] = part.astype(BF16)
        low_t[:, rows] = part.T.astype(BF16)
    for copy in copies[3:]:
        copy.wait()

    kinds = [jnp.where(core == 0, KINDS[0][b], KINDS[1][b]) for b in range(6)]
    for b, kind in enumerate(kinds):
        at = pl.multiple_of((2 * core + b // 3) * TILE, TILE)
        mine = up[kind, :, pl.ds(at, TILE)]
        up_here[:, b * TILE : (b + 1) * TILE] = mine
        (up0, up1)[b // 3][:, pl.ds(pl.multiple_of(kind * TILE, TILE), TILE)] = mine
    for n in range(3):
        for g in range(2 if n == 0 else 0):
            for i in range(16):
                to = (16 * g + i) * COLS
                w[to : to + COLS, :] = spread[i, g * COLS : (g + 1) * COLS, :]
        for rows in tiles:
            raw = rows_dot(x[rows, :], w[bands[n], :]) + dot(low[rows, :], up_here[:, bands[n]])
            for b in (2 * n, 2 * n + 1):
                kind, qkv = kinds[b], (qkv0, qkv1)[b // 3]
                plain = kind == 2
                gain = jnp.where(kind == 0, gains[0:1, :], jnp.where(plain, 1.0, gains[1:2, :]))
                for i in range(GROUP):
                    at = (b - 2 * n) * TILE + i * DIM
                    part = raw[:, at : at + DIM]
                    inv = lax.rsqrt(jnp.mean(part * part, axis=-1, keepdims=True) + EPSILON)
                    inverse[rows, b * GROUP + i : b * GROUP + i + 1] = inv
                    value = part * (jnp.where(plain, 1.0, inv) * gain)
                    to = pl.multiple_of(kind * TILE + i * DIM, DIM)
                    qkv[rows, pl.ds(to, DIM)] = value.astype(BF16)


def project(place, xo, xb, xh, pieces, down, up, gains):
    tokens = 3 * TILE
    whole = pl.BlockSpec(memory_space=pltpu.VMEM)
    far = pl.BlockSpec(memory_space=pl.ANY)
    return pl.pallas_call(
        project_kernel,
        in_specs=[SMEM] + [far] * 8 + [whole] * 3,
        out_specs=[whole] * 6,
        scratch_shapes=[
            pltpu.VMEM((tokens, FEATURES), BF16),
            pltpu.VMEM((16, ROWS, FEATURES), BF16),
            pltpu.VMEM((6 * TILE, FEATURES), BF16),
            pltpu.VMEM((tokens, RANK), BF16),
            pltpu.VMEM((RANK, 6 * TILE), BF16),
            pltpu.SemaphoreType.DMA((19,)),
        ],
        out_shape=[shaped(tokens, 3 * TILE)] * 2
        + [shaped(tokens, DIM, dtype=F32), shaped(RANK, tokens)]
        + [shaped(RANK, 3 * TILE)] * 2,
        compiler_params=pltpu.CompilerParams(vmem_limit_bytes=56 << 20),
        cost_estimate=CHEAP,
        name="project",
    )(place, xo, xb, xh, *pieces, down, up, gains)


def column_of(inverse, at, rows):
    lane = lax.broadcasted_iota(jnp.int32, (rows, DIM), 1)
    return jnp.sum(jnp.where(lane == at, inverse, 0.0), axis=-1, keepdims=True)


def norm_grad(grad, rounded, gain, inv):
    held = rounded.astype(F32)
    along = jnp.mean(held * grad, axis=-1, keepdims=True)
    return inv * (gain * grad - (held / gain) * along)


def exps_of(key, query):
    return jnp.exp2(rows_dot(key, query) * (SCALE * LOG2E))


def attend_kernel(wide, q, k, v, cot, inverse, gains, out, stats, grad_q, grad_k, grad_v):
    h = pl.program_id(0)
    own = 2 * TILE

    def finish_rows(rows, out_t, delta, inv_sum, grad_t):
        out[rows, :] = out_t.T.astype(BF16)
        inv = column_of(inverse[rows, :], wide[GROUP] + h, rows.stop - rows.start)
        grad_q[rows, :] = norm_grad(grad_t.T, q[rows, :], gains[0:1, :], inv).astype(BF16)

    @pl.when(wide[h] > 0)
    def _():
        key_t = k[...].astype(F32).T.astype(BF16)
        value_t = v[...].astype(F32).T.astype(BF16)
        query, cot_in = q[...], cot[...]
        cot_t = cot_in.astype(F32).T
        exps = exps_of(k[:own, :], query)
        exps_far = exps_of(k[own:, :], query[TILE:])
        total = jnp.sum(exps, axis=0, keepdims=True)
        total_far = jnp.sum(exps_far, axis=0, keepdims=True)
        total = total + jnp.concatenate([jnp.zeros_like(total_far), total_far], axis=1)
        inv_sum = 1.0 / total
        probs, probs_far = exps * inv_sum, exps_far * inv_sum[:, TILE:]
        rounded, rounded_far = probs.astype(BF16), probs_far.astype(BF16)
        out_t = dot(value_t[:, :own], rounded)
        out_far = dot(value_t[:, own:], rounded_far)
        out_t = out_t + jnp.concatenate([jnp.zeros_like(out_far), out_far], axis=1)
        out_t = out_t.astype(BF16).astype(F32)
        delta = jnp.sum(cot_t * out_t, axis=0, keepdims=True)
        scores = (probs * (rows_dot(v[:own, :], cot_in) - delta)).astype(BF16)
        scores_far = (probs_far * (rows_dot(v[own:, :], cot_in[TILE:]) - delta[:, TILE:])).astype(BF16)
        grad_t = dot(key_t[:, :own], scores)
        grad_far = dot(key_t[:, own:], scores_far)
        grad_t = (grad_t + jnp.concatenate([jnp.zeros_like(grad_far), grad_far], axis=1)) * SCALE
        grad_k[...] = dot(scores, query) * SCALE
        grad_v[...] = dot(rounded, cot_in)
        stats[0, 0:1, :] = inv_sum[:, TILE:]
        stats[0, 1:2, :] = delta[:, TILE:]
        finish_rows(slice(0, own), out_t, delta, inv_sum, grad_t)

    @pl.when(wide[h] == 0)
    def _():
        stats[...] = jnp.zeros_like(stats)
        for tile in range(2):
            rows = slice(tile * TILE, (tile + 1) * TILE)
            query, key, value, cot_in = q[rows, :], k[rows, :], v[rows, :], cot[rows, :]
            exps = exps_of(key, query)
            inv_sum = 1.0 / jnp.sum(exps, axis=0, keepdims=True)
            probs = exps * inv_sum
            rounded = probs.astype(BF16)
            out_t = dot(value.astype(F32).T.astype(BF16), rounded).astype(BF16).astype(F32)
            delta = jnp.sum(cot_in.astype(F32).T * out_t, axis=0, keepdims=True)
            scores = (probs * (rows_dot(value, cot_in) - delta)).astype(BF16)
            grad_t = dot(key.astype(F32).T.astype(BF16), scores) * SCALE
            grad_k[rows, :] = dot(scores, query) * SCALE
            grad_v[rows, :] = dot(rounded, cot_in)
            finish_rows(rows, out_t, delta, inv_sum, grad_t)


def finish_kernel(
    wide, q, k, v, cot, stats, inverse, gains, part_k, part_v, grad_q,
    low_t, up_q, up_k, up_v, *refs,
):
    *before, sums, result, sum_k, sum_v, rank_t = refs
    h = pl.program_id(0)

    @pl.when(h == 0)
    def _():
        rank_t[...] = before[0][...] if before else jnp.zeros_like(rank_t)

    sum_k[...] = part_k[...]
    sum_v[...] = part_v[...]

    @pl.when(wide[h] > 0)
    def _():
        query, cot_in = q[...], cot[...]
        key, value = k[TILE:, :], v[TILE:, :]
        probs = exps_of(key, query) * stats[0, 0:1, :]
        scores = (probs * (rows_dot(value, cot_in) - stats[0, 1:2, :])).astype(BF16)
        sum_k[TILE:, :] += dot(scores, query) * SCALE
        sum_v[TILE:, :] += dot(probs.astype(BF16), cot_in)

    inv = column_of(inverse[...], wide[GROUP + 1] + h, 2 * TILE)
    grad_k = norm_grad(sum_k[...], k[...], gains[1:2, :], inv).astype(BF16)
    grad_v = sum_v[...].astype(BF16)
    left = low_t[...]
    for kind, grad in enumerate((grad_q[...], grad_k, grad_v)):
        at = pl.multiple_of(kind * TILE + h * DIM, DIM)
        sums[:, pl.ds(at, DIM)] = dot(left, grad).astype(BF16)
    rank_t[...] += (
        rows_dot(up_q[...], grad_q[...]) + rows_dot(up_k[...], grad_k) + rows_dot(up_v[...], grad_v)
    )

    @pl.when(h == GROUP - 1)
    def _():
        if before:
            _, xo, xb = before
            outer = rank_t[:, :TILE].astype(BF16)
            inner = rank_t[:, TILE:].astype(BF16)
            result[...] = (dot(outer, xo[...]) + dot(inner, xb[...])).astype(BF16)
        else:
            result[...] = rank_t[...]


SMEM = pl.BlockSpec(memory_space=pltpu.SMEM)
CHEAP = pl.CostEstimate(flops=1 << 20, bytes_accessed=1 << 16, transcendentals=0)
PARAMS = pltpu.CompilerParams(vmem_limit_bytes=56 << 20)


def per_head(rows, at=0, block=0):
    return pl.BlockSpec((rows, DIM), lambda h: (block, at + h))


def constant(*shape):
    return pl.BlockSpec(shape, lambda h: (0,) * len(shape))


def shaped(*shape, dtype=BF16):
    return jax.ShapeDtypeStruct(shape, dtype)


def attend(wide, qkv, cot, inverse, gains):
    own = 2 * TILE
    return pl.pallas_call(
        attend_kernel,
        grid=(GROUP,),
        in_specs=[
            SMEM,
            per_head(own),
            per_head(3 * TILE, GROUP),
            per_head(3 * TILE, 2 * GROUP),
            per_head(own),
            constant(own, DIM),
            constant(2, DIM),
        ],
        out_specs=[
            per_head(own),
            pl.BlockSpec((1, 2, TILE), lambda h: (h, 0, 0)),
            per_head(own),
            per_head(own),
            per_head(own),
        ],
        out_shape=[
            shaped(own, GROUP * DIM),
            shaped(GROUP, 2, TILE, dtype=F32),
            shaped(own, GROUP * DIM),
            shaped(own, GROUP * DIM, dtype=F32),
            shaped(own, GROUP * DIM, dtype=F32),
        ],
        compiler_params=PARAMS,
        cost_estimate=CHEAP,
        name="attend",
    )(wide, qkv, qkv, qkv, cot, inverse, gains)


def finish(wide, qkv, cot, stats, inverse, gains, part_k, part_v, grad_q, low_t, up, *before):
    own = 2 * TILE
    result = (
        shaped(RANK, FEATURES) if before else shaped(RANK, own, dtype=F32)
    )
    return pl.pallas_call(
        finish_kernel,
        grid=(GROUP,),
        in_specs=[
            SMEM,
            per_head(TILE, 0, 2),
            per_head(own, GROUP),
            per_head(own, 2 * GROUP),
            per_head(TILE),
            pl.BlockSpec((1, 2, TILE), lambda h: (h, 0, 0)),
            constant(own, DIM),
            constant(2, DIM),
            per_head(own),
            per_head(own),
            per_head(own),
            constant(RANK, own),
            per_head(RANK),
            per_head(RANK, GROUP),
            per_head(RANK, 2 * GROUP),
        ]
        + [constant(*array.shape) for array in before],
        out_specs=[constant(RANK, 3 * TILE), constant(*result.shape)],
        out_shape=[
            shaped(RANK, 3 * TILE),
            result,
        ],
        scratch_shapes=[
            pltpu.VMEM((own, DIM), F32),
            pltpu.VMEM((own, DIM), F32),
            pltpu.VMEM((RANK, own), F32),
        ],
        compiler_params=PARAMS,
        cost_estimate=CHEAP,
        name="finish",
    )(
        wide, qkv, qkv, qkv, cot, stats, inverse, gains, part_k, part_v, grad_q,
        low_t, up, up, up, *before,
    )


def swap(block, axis):
    return lax.ppermute(block, axis, [(0, 1), (1, 0)])


def hop(block, axis, count, step):
    return lax.ppermute(block, axis, [(i, (i + step) % count) for i in range(count)])


def from_above(block, stage, distance):
    pairs = []
    for core in range(2):
        for i in range(4):
            for j in range(4):
                above = (j + distance) % 4
                if core == stage:
                    pairs.append((16 * core + 4 * i + above, 16 * core + 4 * i + j))
                else:
                    pairs.append((16 * core + 4 * above + i, 16 * core + 4 * j + i))
    return lax.ppermute(block, ("c", "y", "x"), pairs)


def pick(options, at):
    out = options[0]
    for i in range(1, len(options)):
        out = jnp.where(at == i, options[i], out)
    return out


def along_z(block, stride):
    pairs = []
    for source in range(8):
        target = (source + stride) % 8
        pairs.append((ring_index(source, 0), ring_index(target, 0)))
        pairs.append((ring_index(target, 1), ring_index(source, 1)))
    return lax.ppermute(block, ("zh", "c", "zl"), pairs)


def ring_index(z, core):
    return (z // 4) * 8 + core * 4 + z % 4


def gather_first(packed, ready):
    core, zl = lax.axis_index("c"), lax.axis_index("zl")
    spot = lax.axis_index("y") * 4 + lax.axis_index("x")
    along = ("zh", "zl")
    planes = [packed, hop(packed, along, 8, -1), hop(packed, along, 8, 2), hop(packed, along, 8, 1)]
    planes, ready = lax.optimization_barrier((planes, ready))
    third = (spot * COLS + lax.broadcasted_iota(jnp.int32, (COLS, 1), 0)) // TILE
    first = jnp.where(core == 0, pick([0, 1, 2], third), pick([2, 3, 0], third))
    second = jnp.where(core == 0, pick([3, 0, 1], third), pick([1, 2, 3], third))
    columns, small = [plane[:COLS] for plane in planes], [plane[COLS:] for plane in planes]
    block = jnp.concatenate(
        [pick(columns, lax.rem(group - zl + 4, 4)) for group in (first, second)]
        + [pick(small, lax.rem(plane - zl + 4, 4)) for plane in range(4)]
    )
    return block, *ready


def gather_plane(block, crossing):
    core, y, x = (lax.axis_index(axis) for axis in ("c", "y", "x"))
    inner, outer = jnp.where(core == 0, x, y), jnp.where(core == 0, y, x)
    ring = jnp.zeros((4,) + block.shape, block.dtype)
    for distance in range(4):
        piece = from_above(block, 0, distance) if distance else block
        ring = lax.dynamic_update_index_in_dim(ring, piece, lax.rem(inner + distance, 4), 0)
    above, below = from_above(ring, 1, 1), from_above(ring, 1, 3)
    far = [from_above(above[:2], 1, 1), from_above(below[2:], 1, 3)]
    crossing = lax.optimization_barrier((crossing, above, below))[0]
    pieces = [ring, above, below, *far]
    rest = jnp.zeros((4, 4, ROWS - 2 * COLS, FEATURES), BF16)
    for distance, j, piece in zip((0, 1, 3, 2, 2), (0, 0, 0, 0, 2), pieces):
        at = lax.rem(outer + distance, 4)
        rest = lax.dynamic_update_slice(rest, piece[None, :, 2 * COLS :], (at, j, 0, 0))
    rest = jnp.where(core == 0, rest, jnp.swapaxes(rest, 0, 1))
    return outer, pieces, rest, crossing


def reduce_adapter(first, second, out_down):
    core = lax.axis_index("c")
    width = GROUP * DIM
    down = out_down.reshape(RANK, 64, FEATURES // 64).transpose(1, 2, 0).reshape(64, FEATURES)
    payload = jnp.concatenate([first, second, down], axis=1)
    parts = lax.all_to_all(payload, FSDP, 0, 0, tiled=True)
    mine = jnp.sum(parts.astype(F32), axis=0).reshape(-1, DIM)
    every = lax.all_gather(mine, ("zh", "c")).reshape(2, 2, -1)
    both = every[0] + every[1]
    grad_up = jnp.concatenate(
        [
            both[side, (3 * group + kind) * width : (3 * group + kind + 1) * width]
            for kind in range(3)
            for side in range(2)
            for group in range(2)
        ]
    )
    grad_down = (both[0] + both[1])[6 * width :]
    return grad_down.reshape(FEATURES // 64, RANK), grad_up.reshape(1, -1)


def local(hidden, modulation, cotangent, frozen, down, up, gains, windows):
    high, core = lax.axis_index("zh"), lax.axis_index("c")
    outermost = core == high
    packed = jnp.concatenate([frozen.T, down.reshape(1, FEATURES), up.reshape(3, FEATURES)])
    packed, hidden = lax.optimization_barrier((packed, hidden))
    own = modulated_norm(hidden[0], modulation[0])
    other = swap(own, "c")
    width = HALF * DIM
    cot_own = lax.dynamic_slice(cotangent[0], (0, core * width), (TILE, width))
    cot_other = swap(lax.dynamic_slice(cotangent[0], (0, (1 - core) * width), (TILE, width)), "c")
    xo = jnp.where(outermost, own, other)
    xb = jnp.where(outermost, other, own)
    half = lax.dynamic_slice(xb, (core * (TILE // 2), 0), (TILE // 2, FEATURES))
    block, half, cot_other = gather_first(packed, (half, cot_other))
    cot_edge = jnp.where(outermost, cot_other, cot_own)
    outer, pieces, rest, near = gather_plane(block, swap(half, "zh"))
    far = swap(near, "c")
    xh = jnp.concatenate([jnp.where(core == 0, near, far), jnp.where(core == 0, far, near)])
    cot = jnp.concatenate([jnp.where(outermost, cot_own, cot_other), cot_edge])

    wide = (lax.dynamic_slice(windows, (core * HALF,), (HALF,)) > 1).astype(jnp.int32)
    xh, cot_edge = lax.optimization_barrier((xh, cot_edge))
    cot_halo = swap(cot_edge, "zh")
    small = rest.reshape(16, 4, 4, FEATURES).transpose(2, 1, 0, 3).reshape(4, 64, FEATURES)
    qkv0, qkv1, inverse, low_t, up0, up1 = project(
        jnp.stack([core, outer]), xo, xb, xh, pieces,
        small[0].reshape(FEATURES, RANK), small[1:], gains,
    )
    groups = (qkv0, up0), (qkv1, up1)

    heads = []
    for g in range(2):
        lanes = [
            GROUP * jnp.where(core == 0, *(KINDS[c].index(kind, 3 * g, 3 * g + 3) for c in (0, 1)))
            for kind in (0, 1)
        ]
        heads.append(jnp.stack([*wide[GROUP * g : GROUP * (g + 1)], *lanes]).astype(jnp.int32))
    back, kept, sums = [], [], []
    held, exchanged = [], []
    for g, (qkv, _) in enumerate(groups):
        cot_g = cot[:, g * GROUP * DIM : (g + 1) * GROUP * DIM]
        out, stats, grad_q, part_k, part_v = attend(heads[g], qkv, cot_g, inverse, gains)
        tiles = out[:TILE], out[TILE:]
        back.append(swap(jnp.where(outermost, tiles[1], tiles[0]), "c"))
        kept.append(jnp.where(outermost, tiles[0], tiles[1]))
        held.append((*groups[g], stats, part_k, part_v, grad_q))
        exchanged.append(swap(stats, "zh"))
    held = lax.optimization_barrier(held)
    for g, (qkv, up_mine, _, part_k, part_v, grad_q) in enumerate(held):
        part, result = finish(
            heads[g], qkv, cot_halo[:, g * GROUP * DIM : (g + 1) * GROUP * DIM], exchanged[g], inverse, gains, part_k, part_v, grad_q, low_t, up_mine, *([result, xo, xb] if g else []),
        )
        sums.append(part)
    sides = [jnp.where(core == side, kept[g], back[g]) for side in range(2) for g in range(2)]
    attn_out = jnp.concatenate(sides, axis=1)
    grad_down, grad_up = reduce_adapter(sums[0], sums[1], result)
    return attn_out[None], grad_down, grad_up


def solution(mesh):
    split = Mesh(mesh.devices.reshape(2, 2, 4, 4, 4), AXES)
    sp = ("zh", "c")
    in_specs = (
        P(FSDP, sp, None),
        P(FSDP, None, None),
        P(FSDP, sp, None),
        P(None, FSDP),
        P(FSDP, None),
        P(FSDP, None),
        P(),
        P(),
    )
    out_specs = (P(FSDP, sp, None), P(FSDP, None), P(FSDP, None))
    return jax.shard_map(local, mesh=split, in_specs=in_specs, out_specs=out_specs, check_vma=False)
```

```python
import functools
import math

import jax
import jax.numpy as jnp
from jax import lax
from jax.experimental import pallas as pl
from jax.experimental.pallas import tpu as pltpu
from jax.sharding import Mesh, PartitionSpec as P

HEADS = 12
HALF = 6
DIM = 128
TILE = 384
FEATURES = 1536
RANK = 64
COLS = 72
ROWS = 2 * COLS + 16
PIECES = (0, 0), (1, 0), (3, 0), (2, 0), (2, 2)
KINDS = (0, 1, 2, 2, 0, 1), (1, 2, 0, 0, 1, 2)
GROUP = 3
EPSILON = 1e-06
SCALE = DIM**-0.5
LOG2E = math.log2(math.e)
AXES = ("zh", "c", "zl", "y", "x")
FSDP = ("zl", "y", "x")
NT = (((1,), (1,)), ((), ()))
F32 = jnp.float32
BF16 = jnp.bfloat16


def rows_dot(a, b):
    return lax.dot_general(a, b, NT, preferred_element_type=F32)


def dot(a, b):
    return jnp.dot(a, b, preferred_element_type=F32)


def norm_kernel(hidden, modulation, out):
    wide = hidden[...].astype(F32)
    centred = wide - jnp.mean(wide, axis=-1, keepdims=True)
    variance = jnp.mean(centred * centred, axis=-1, keepdims=True)
    unit = centred * lax.rsqrt(variance + EPSILON)
    out[...] = (unit * (1.0 + modulation[0:1, :]) + modulation[1:2, :]).astype(BF16)


def modulated_norm(hidden, modulation):
    rows = 128
    return pl.pallas_call(
        norm_kernel,
        grid=(TILE // rows,),
        in_specs=[
            pl.BlockSpec((rows, FEATURES), lambda i: (i, 0)),
            pl.BlockSpec((2, FEATURES), lambda i: (0, 0)),
        ],
        out_specs=pl.BlockSpec((rows, FEATURES), lambda i: (i, 0)),
        out_shape=jax.ShapeDtypeStruct((TILE, FEATURES), BF16),
        compiler_params=pltpu.CompilerParams(vmem_limit_bytes=32 << 20),
        name="modulated_norm",
    )(hidden, modulation)


def project_kernel(
    place, xo, xb, xh, *refs,
):
    *pieces, gains, qkv0, qkv1, inverse, low_t, up0, up1 = refs[:12]
    x, spread, w, low, up_here, down, rest, sems = refs[12:]
    core, outer, inner = place[0], place[1], place[2]
    wide = 2 * TILE
    tiles = [slice(m * TILE, (m + 1) * TILE) for m in range(3)]
    bands = [slice(n * wide, (n + 1) * wide) for n in range(3)]
    copies = [
        pltpu.make_async_copy(tile, x.at[rows, :], sems.at[m])
        for m, (tile, rows) in enumerate(zip((xo, xb, xh), tiles))
    ]
    for (distance, first), piece in zip(PIECES, pieces):
        i = lax.rem(outer + distance, 4)
        for k in range(piece.shape[0]):
            j = lax.rem(inner + first + k, 4)
            slot = jnp.where(core == 0, 4 * i + j, 4 * j + i)
            sem = sems.at[len(copies)]
            copies.append(pltpu.make_async_copy(piece.at[k], spread.at[slot], sem))
    for copy in copies:
        copy.start()
    inverse[...] = jnp.zeros_like(inverse)
    for copy in copies:
        copy.wait()
    for i in range(16):
        rest[16 * i : 16 * (i + 1), :] = spread[i, 2 * COLS :, :]
    to = lax.broadcasted_iota(jnp.int32, (64, 256), 0)
    source = 16 * (to % 16) + 4 * (to // 16)
    at_column = lax.broadcasted_iota(jnp.int32, (64, 256), 1)

    def adapter_rows(r):
        return dot(jnp.where(at_column == source + r, 1.0, 0.0).astype(BF16), rest[...])

    flat = adapter_rows(0)
    for i in range(24):
        part = flat[:, RANK * i : RANK * (i + 1)]
        down[pl.ds(i, 64, stride=24), :] = jnp.concatenate([part, part], axis=1)
    down_here = down[:, :RANK].astype(BF16)
    up = [adapter_rows(1 + kind).astype(BF16) for kind in range(3)]
    for m, rows in enumerate(tiles):
        part = dot(x[rows, :], down_here)
        low[rows, :] = part.astype(BF16)
        low_t[:, rows] = part.T.astype(BF16)
    kinds = [jnp.where(core == 0, KINDS[0][b], KINDS[1][b]) for b in range(6)]
    for b, kind in enumerate(kinds):
        mine = jnp.zeros((RANK, TILE), BF16)
        for c in range(2):
            at = (2 * c + b // 3) * TILE
            mine = jnp.where(core == c, up[KINDS[c][b]][:, at : at + TILE], mine)
        up_here[:, b * TILE : (b + 1) * TILE] = mine
        (up0, up1)[b // 3][:, pl.ds(pl.multiple_of(kind * TILE, TILE), TILE)] = mine
    for n in range(3):
        for g in range(2 if n == 0 else 0):
            for i in range(16):
                to = (16 * g + i) * COLS
                w[to : to + COLS, :] = spread[i, g * COLS : (g + 1) * COLS, :]
        for rows in tiles:
            raw = rows_dot(x[rows, :], w[bands[n], :]) + dot(low[rows, :], up_here[:, bands[n]])
            for b in (2 * n, 2 * n + 1):
                kind, qkv = kinds[b], (qkv0, qkv1)[b // 3]
                plain = kind == 2
                gain = jnp.where(kind == 0, gains[0:1, :], jnp.where(plain, 1.0, gains[1:2, :]))
                for i in range(GROUP):
                    at = (b - 2 * n) * TILE + i * DIM
                    part = raw[:, at : at + DIM]
                    inv = lax.rsqrt(jnp.mean(part * part, axis=-1, keepdims=True) + EPSILON)
                    inverse[rows, b * GROUP + i : b * GROUP + i + 1] = inv
                    value = part * (jnp.where(plain, 1.0, inv) * gain)
                    to = pl.multiple_of(kind * TILE + i * DIM, DIM)
                    qkv[rows, pl.ds(to, DIM)] = value.astype(BF16)


def project(place, xo, xb, xh, pieces, gains):
    tokens = 3 * TILE
    whole = pl.BlockSpec(memory_space=pltpu.VMEM)
    far = pl.BlockSpec(memory_space=pl.ANY)
    return pl.pallas_call(
        project_kernel,
        in_specs=[SMEM] + [far] * 8 + [whole],
        out_specs=[whole] * 6,
        scratch_shapes=[
            pltpu.VMEM((tokens, FEATURES), BF16),
            pltpu.VMEM((16, ROWS, FEATURES), BF16),
            pltpu.VMEM((6 * TILE, FEATURES), BF16),
            pltpu.VMEM((tokens, RANK), BF16),
            pltpu.VMEM((RANK, 6 * TILE), BF16),
            pltpu.VMEM((FEATURES, DIM), F32),
            pltpu.VMEM((256, FEATURES), BF16),
            pltpu.SemaphoreType.DMA((19,)),
        ],
        out_shape=[shaped(tokens, 3 * TILE)] * 2
        + [shaped(tokens, DIM, dtype=F32), shaped(RANK, tokens)]
        + [shaped(RANK, 3 * TILE)] * 2,
        compiler_params=pltpu.CompilerParams(vmem_limit_bytes=56 << 20),
        cost_estimate=CHEAP,
        name="project",
    )(place, xo, xb, xh, *pieces, gains)


def column_of(inverse, at, rows):
    lane = lax.broadcasted_iota(jnp.int32, (rows, DIM), 1)
    return jnp.sum(jnp.where(lane == at, inverse, 0.0), axis=-1, keepdims=True)


def norm_grad(grad, rounded, gain, inv):
    held = rounded.astype(F32)
    along = jnp.mean(held * grad, axis=-1, keepdims=True)
    return inv * (gain * grad - (held / gain) * along)


def exps_of(key, query):
    return jnp.exp2(rows_dot(key, query) * (SCALE * LOG2E))


def attend_kernel(wide, q, k, v, cot, inverse, gains, out, stats, grad_q, grad_k, grad_v):
    h = pl.program_id(0)
    own = 2 * TILE

    def finish_rows(rows, out_t, delta, inv_sum, grad_t):
        out[rows, :] = out_t.T.astype(BF16)
        inv = column_of(inverse[rows, :], wide[GROUP] + h, rows.stop - rows.start)
        grad_q[rows, :] = norm_grad(grad_t.T, q[rows, :], gains[0:1, :], inv).astype(BF16)

    @pl.when(wide[h] > 0)
    def _():
        key_t = k[...].astype(F32).T.astype(BF16)
        value_t = v[...].astype(F32).T.astype(BF16)
        query, cot_in = q[...], cot[...]
        cot_t = cot_in.astype(F32).T
        exps = exps_of(k[:own, :], query)
        exps_far = exps_of(k[own:, :], query[TILE:])
        total = jnp.sum(exps, axis=0, keepdims=True)
        total_far = jnp.sum(exps_far, axis=0, keepdims=True)
        total = total + jnp.concatenate([jnp.zeros_like(total_far), total_far], axis=1)
        inv_sum = 1.0 / total
        probs, probs_far = exps * inv_sum, exps_far * inv_sum[:, TILE:]
        rounded, rounded_far = probs.astype(BF16), probs_far.astype(BF16)
        out_t = dot(value_t[:, :own], rounded)
        out_far = dot(value_t[:, own:], rounded_far)
        out_t = out_t + jnp.concatenate([jnp.zeros_like(out_far), out_far], axis=1)
        out_t = out_t.astype(BF16).astype(F32)
        delta = jnp.sum(cot_t * out_t, axis=0, keepdims=True)
        scores = (probs * (rows_dot(v[:own, :], cot_in) - delta)).astype(BF16)
        scores_far = (probs_far * (rows_dot(v[own:, :], cot_in[TILE:]) - delta[:, TILE:])).astype(BF16)
        grad_t = dot(key_t[:, :own], scores)
        grad_far = dot(key_t[:, own:], scores_far)
        grad_t = (grad_t + jnp.concatenate([jnp.zeros_like(grad_far), grad_far], axis=1)) * SCALE
        grad_k[...] = dot(scores, query) * SCALE
        grad_v[...] = dot(rounded, cot_in)
        stats[0, 0:1, :] = inv_sum[:, TILE:]
        stats[0, 1:2, :] = delta[:, TILE:]
        finish_rows(slice(0, own), out_t, delta, inv_sum, grad_t)

    @pl.when(wide[h] == 0)
    def _():
        stats[...] = jnp.zeros_like(stats)
        for tile in range(2):
            rows = slice(tile * TILE, (tile + 1) * TILE)
            query, key, value, cot_in = q[rows, :], k[rows, :], v[rows, :], cot[rows, :]
            exps = exps_of(key, query)
            inv_sum = 1.0 / jnp.sum(exps, axis=0, keepdims=True)
            probs = exps * inv_sum
            rounded = probs.astype(BF16)
            out_t = dot(value.astype(F32).T.astype(BF16), rounded).astype(BF16).astype(F32)
            delta = jnp.sum(cot_in.astype(F32).T * out_t, axis=0, keepdims=True)
            scores = (probs * (rows_dot(value, cot_in) - delta)).astype(BF16)
            grad_t = dot(key.astype(F32).T.astype(BF16), scores) * SCALE
            grad_k[rows, :] = dot(scores, query) * SCALE
            grad_v[rows, :] = dot(rounded, cot_in)
            finish_rows(rows, out_t, delta, inv_sum, grad_t)


def finish_kernel(
    wide, q, k, v, cot, stats, inverse, gains, part_k, part_v, grad_q,
    low_t, up_q, up_k, up_v, *refs,
):
    *before, sums, result, sum_k, sum_v, rank_t = refs
    h = pl.program_id(0)

    @pl.when(h == 0)
    def _():
        rank_t[...] = before[0][...] if before else jnp.zeros_like(rank_t)

    sum_k[...] = part_k[...]
    sum_v[...] = part_v[...]

    @pl.when(wide[h] > 0)
    def _():
        query, cot_in = q[...], cot[...]
        key, value = k[TILE:, :], v[TILE:, :]
        probs = exps_of(key, query) * stats[0, 0:1, :]
        scores = (probs * (rows_dot(value, cot_in) - stats[0, 1:2, :])).astype(BF16)
        sum_k[TILE:, :] += dot(scores, query) * SCALE
        sum_v[TILE:, :] += dot(probs.astype(BF16), cot_in)

    inv = column_of(inverse[...], wide[GROUP + 1] + h, 2 * TILE)
    grad_k = norm_grad(sum_k[...], k[...], gains[1:2, :], inv).astype(BF16)
    grad_v = sum_v[...].astype(BF16)
    left = low_t[...]
    for kind, grad in enumerate((grad_q[...], grad_k, grad_v)):
        at = pl.multiple_of(kind * TILE + h * DIM, DIM)
        sums[:, pl.ds(at, DIM)] = dot(left, grad).astype(BF16)
    rank_t[...] += (
        rows_dot(up_q[...], grad_q[...]) + rows_dot(up_k[...], grad_k) + rows_dot(up_v[...], grad_v)
    )

    @pl.when(h == GROUP - 1)
    def _():
        if before:
            _, xo, xb = before
            outer = rank_t[:, :TILE].astype(BF16)
            inner = rank_t[:, TILE:].astype(BF16)
            result[...] = (dot(outer, xo[...]) + dot(inner, xb[...])).astype(BF16)
        else:
            result[...] = rank_t[...]


SMEM = pl.BlockSpec(memory_space=pltpu.SMEM)
CHEAP = pl.CostEstimate(flops=1 << 20, bytes_accessed=1 << 16, transcendentals=0)
PARAMS = pltpu.CompilerParams(vmem_limit_bytes=56 << 20)


def per_head(rows, at=0, block=0):
    return pl.BlockSpec((rows, DIM), lambda h: (block, at + h))


def constant(*shape):
    return pl.BlockSpec(shape, lambda h: (0,) * len(shape))


def shaped(*shape, dtype=BF16):
    return jax.ShapeDtypeStruct(shape, dtype)


def attend(wide, qkv, cot, inverse, gains):
    own = 2 * TILE
    return pl.pallas_call(
        attend_kernel,
        grid=(GROUP,),
        in_specs=[
            SMEM,
            per_head(own),
            per_head(3 * TILE, GROUP),
            per_head(3 * TILE, 2 * GROUP),
            per_head(own),
            constant(own, DIM),
            constant(2, DIM),
        ],
        out_specs=[
            per_head(own),
            pl.BlockSpec((1, 2, TILE), lambda h: (h, 0, 0)),
            per_head(own),
            per_head(own),
            per_head(own),
        ],
        out_shape=[
            shaped(own, GROUP * DIM),
            shaped(GROUP, 2, TILE, dtype=F32),
            shaped(own, GROUP * DIM),
            shaped(own, GROUP * DIM, dtype=F32),
            shaped(own, GROUP * DIM, dtype=F32),
        ],
        compiler_params=PARAMS,
        cost_estimate=CHEAP,
        name="attend",
    )(wide, qkv, qkv, qkv, cot, inverse, gains)


def finish(wide, qkv, cot, stats, inverse, gains, part_k, part_v, grad_q, low_t, up, *before):
    own = 2 * TILE
    result = (
        shaped(RANK, FEATURES) if before else shaped(RANK, own, dtype=F32)
    )
    return pl.pallas_call(
        finish_kernel,
        grid=(GROUP,),
        in_specs=[
            SMEM,
            per_head(TILE, 0, 2),
            per_head(own, GROUP),
            per_head(own, 2 * GROUP),
            per_head(TILE),
            pl.BlockSpec((1, 2, TILE), lambda h: (h, 0, 0)),
            constant(own, DIM),
            constant(2, DIM),
            per_head(own),
            per_head(own),
            per_head(own),
            constant(RANK, own),
            per_head(RANK),
            per_head(RANK, GROUP),
            per_head(RANK, 2 * GROUP),
        ]
        + [constant(*array.shape) for array in before],
        out_specs=[constant(RANK, 3 * TILE), constant(*result.shape)],
        out_shape=[
            shaped(RANK, 3 * TILE),
            result,
        ],
        scratch_shapes=[
            pltpu.VMEM((own, DIM), F32),
            pltpu.VMEM((own, DIM), F32),
            pltpu.VMEM((RANK, own), F32),
        ],
        compiler_params=PARAMS,
        cost_estimate=CHEAP,
        name="finish",
    )(
        wide, qkv, qkv, qkv, cot, stats, inverse, gains, part_k, part_v, grad_q,
        low_t, up, up, up, *before,
    )


def swap(block, axis):
    return lax.ppermute(block, axis, [(0, 1), (1, 0)])


def hop(block, axis, count, step):
    return lax.ppermute(block, axis, [(i, (i + step) % count) for i in range(count)])


def from_above(block, stage, distance):
    pairs = []
    for core in range(2):
        for i in range(4):
            for j in range(4):
                above = (j + distance) % 4
                if core == stage:
                    pairs.append((16 * core + 4 * i + above, 16 * core + 4 * i + j))
                else:
                    pairs.append((16 * core + 4 * above + i, 16 * core + 4 * j + i))
    return lax.ppermute(block, ("c", "y", "x"), pairs)


def pick(options, at):
    out = options[0]
    for i in range(1, len(options)):
        out = jnp.where(at == i, options[i], out)
    return out


def along_z(block, stride):
    pairs = []
    for source in range(8):
        target = (source + stride) % 8
        pairs.append((ring_index(source, 0), ring_index(target, 0)))
        pairs.append((ring_index(target, 1), ring_index(source, 1)))
    return lax.ppermute(block, ("zh", "c", "zl"), pairs)


def ring_index(z, core):
    return (z // 4) * 8 + core * 4 + z % 4


def gather_first(packed, ready):
    core, zl = lax.axis_index("c"), lax.axis_index("zl")
    spot = lax.axis_index("y") * 4 + lax.axis_index("x")
    along = ("zh", "zl")
    planes = [packed, hop(packed, along, 8, -1), hop(packed, along, 8, 2), hop(packed, along, 8, 1)]
    planes, ready = lax.optimization_barrier((planes, ready))
    third = (spot * COLS + lax.broadcasted_iota(jnp.int32, (COLS, 1), 0)) // TILE
    first = jnp.where(core == 0, pick([0, 1, 2], third), pick([2, 3, 0], third))
    second = jnp.where(core == 0, pick([3, 0, 1], third), pick([1, 2, 3], third))
    columns, small = [plane[:COLS] for plane in planes], [plane[COLS:] for plane in planes]
    block = jnp.concatenate(
        [pick(columns, lax.rem(group - zl + 4, 4)) for group in (first, second)]
        + [pick(small, lax.rem(plane - zl + 4, 4)) for plane in range(4)]
    )
    return block, ready


def gather_second(ring, crossing):
    above, below = from_above(ring, 1, 1), from_above(ring, 1, 3)
    onward = above[:2], below[2:]
    far = [from_above(onward[0], 1, 1), from_above(onward[1], 1, 3)]
    crossing = lax.optimization_barrier((crossing, *onward))[0]
    return [ring, above, below, *far], crossing


def reduce_adapter(first, second, out_down):
    core = lax.axis_index("c")
    width = GROUP * DIM
    down = out_down.reshape(RANK, 64, FEATURES // 64).transpose(1, 2, 0).reshape(64, FEATURES)
    payload = jnp.concatenate([first, second, down], axis=1)
    parts = lax.all_to_all(payload, FSDP, 0, 0, tiled=True)
    mine = jnp.sum(parts.astype(F32), axis=0).reshape(-1, DIM)
    every = lax.all_gather(mine, ("zh", "c")).reshape(2, 2, -1)
    both = every[0] + every[1]
    grad_up = jnp.concatenate(
        [
            both[side, (3 * group + kind) * width : (3 * group + kind + 1) * width]
            for kind in range(3)
            for side in range(2)
            for group in range(2)
        ]
    )
    grad_down = (both[0] + both[1])[6 * width :]
    return grad_down.reshape(FEATURES // 64, RANK), grad_up.reshape(1, -1)


def local(hidden, modulation, cotangent, frozen, down, up, gains, windows):
    high, core = lax.axis_index("zh"), lax.axis_index("c")
    outermost = core == high
    packed = jnp.concatenate([frozen.T, down.reshape(1, FEATURES), up.reshape(3, FEATURES)])
    packed, hidden = lax.optimization_barrier((packed, hidden))
    own = modulated_norm(hidden[0], modulation[0])
    other = swap(own, "c")
    width = HALF * DIM
    xo = jnp.where(outermost, own, other)
    xb = jnp.where(outermost, other, own)
    half = lax.dynamic_slice(xb, (core * (TILE // 2), 0), (TILE // 2, FEATURES))
    cot_own = lax.dynamic_slice(cotangent[0], (0, core * width), (TILE, width))
    cot_other = swap(lax.dynamic_slice(cotangent[0], (0, (1 - core) * width), (TILE, width)), "c")
    block, (half, cot_other) = gather_first(packed, (half, cot_other))
    ring = [block] + [from_above(block, 0, distance) for distance in (1, 2, 3)]
    ring, near = lax.optimization_barrier((jnp.stack(ring), along_z(half, 1)))
    pieces, near = gather_second(ring, along_z(near, 3))
    far = swap(near, "c")
    xh = jnp.concatenate([jnp.where(core == 0, near, far), jnp.where(core == 0, far, near)])
    cot_edge = jnp.where(outermost, cot_other, cot_own)
    cot = jnp.concatenate([jnp.where(outermost, cot_own, cot_other), cot_edge])

    wide = (lax.dynamic_slice(windows, (core * HALF,), (HALF,)) > 1).astype(jnp.int32)
    xh, cot_edge = lax.optimization_barrier((xh, cot_edge))
    cot_halo = swap(cot_edge, "zh")
    y, x = lax.axis_index("y"), lax.axis_index("x")
    place = jnp.stack([core, jnp.where(core == 0, y, x), jnp.where(core == 0, x, y)])
    qkv0, qkv1, inverse, low_t, up0, up1 = project(place, xo, xb, xh, pieces, gains)
    groups = (qkv0, up0), (qkv1, up1)

    heads = []
    for g in range(2):
        lanes = [
            GROUP * jnp.where(core == 0, *(KINDS[c].index(kind, 3 * g, 3 * g + 3) for c in (0, 1)))
            for kind in (0, 1)
        ]
        heads.append(jnp.stack([*wide[GROUP * g : GROUP * (g + 1)], *lanes]).astype(jnp.int32))
    back, kept, sums = [], [], []
    held, exchanged = [], []
    for g, (qkv, _) in enumerate(groups):
        cot_g = cot[:, g * GROUP * DIM : (g + 1) * GROUP * DIM]
        out, stats, grad_q, part_k, part_v = attend(heads[g], qkv, cot_g, inverse, gains)
        tiles = out[:TILE], out[TILE:]
        back.append(swap(jnp.where(outermost, tiles[1], tiles[0]), "c"))
        kept.append(jnp.where(outermost, tiles[0], tiles[1]))
        held.append((*groups[g], stats, part_k, part_v, grad_q))
        exchanged.append(swap(stats, "zh"))
    held = lax.optimization_barrier(held)
    for g, (qkv, up_mine, _, part_k, part_v, grad_q) in enumerate(held):
        part, result = finish(
            heads[g], qkv, cot_halo[:, g * GROUP * DIM : (g + 1) * GROUP * DIM], exchanged[g], inverse, gains, part_k, part_v, grad_q, low_t, up_mine, *([result, xo, xb] if g else []),
        )
        sums.append(part)
    sides = [jnp.where(core == side, kept[g], back[g]) for side in range(2) for g in range(2)]
    attn_out = jnp.concatenate(sides, axis=1)
    grad_down, grad_up = reduce_adapter(sums[0], sums[1], result)
    return attn_out[None], grad_down, grad_up


def solution(mesh):
    split = Mesh(mesh.devices.reshape(2, 2, 4, 4, 4), AXES)
    sp = ("zh", "c")
    in_specs = (
        P(FSDP, sp, None),
        P(FSDP, None, None),
        P(FSDP, sp, None),
        P(None, FSDP),
        P(FSDP, None),
        P(FSDP, None),
        P(),
        P(),
    )
    out_specs = (P(FSDP, sp, None), P(FSDP, None), P(FSDP, None))
    return jax.shard_map(local, mesh=split, in_specs=in_specs, out_specs=out_specs, check_vma=False)
```

```python
import functools
import math

import jax
import jax.numpy as jnp
from jax import lax
from jax.experimental import pallas as pl
from jax.experimental.pallas import tpu as pltpu
from jax.sharding import Mesh, PartitionSpec as P

HEADS = 12
HALF = 6
DIM = 128
TILE = 384
FEATURES = 1536
RANK = 64
COLS = 72
ROWS = 2 * COLS + 16
PIECES = tuple((distance, first) for distance in (0, 1, 3, 2) for first in (0, 2))
KINDS = (0, 1, 2, 2, 0, 1), (1, 2, 0, 0, 1, 2)
GROUP = 3
EPSILON = 1e-06
SCALE = DIM**-0.5
LOG2E = math.log2(math.e)
AXES = ("zh", "c", "zl", "y", "x")
FSDP = ("zl", "y", "x")
NT = (((1,), (1,)), ((), ()))
F32 = jnp.float32
BF16 = jnp.bfloat16


def rows_dot(a, b):
    return lax.dot_general(a, b, NT, preferred_element_type=F32)


def dot(a, b):
    return jnp.dot(a, b, preferred_element_type=F32)


def norm_kernel(hidden, modulation, out):
    wide = hidden[...].astype(F32)
    centred = wide - jnp.mean(wide, axis=-1, keepdims=True)
    variance = jnp.mean(centred * centred, axis=-1, keepdims=True)
    unit = centred * lax.rsqrt(variance + EPSILON)
    out[...] = (unit * (1.0 + modulation[0:1, :]) + modulation[1:2, :]).astype(BF16)


def modulated_norm(hidden, modulation):
    rows = 128
    return pl.pallas_call(
        norm_kernel,
        grid=(TILE // rows,),
        in_specs=[
            pl.BlockSpec((rows, FEATURES), lambda i: (i, 0)),
            pl.BlockSpec((2, FEATURES), lambda i: (0, 0)),
        ],
        out_specs=pl.BlockSpec((rows, FEATURES), lambda i: (i, 0)),
        out_shape=jax.ShapeDtypeStruct((TILE, FEATURES), BF16),
        compiler_params=pltpu.CompilerParams(vmem_limit_bytes=32 << 20),
        name="modulated_norm",
    )(hidden, modulation)


def project_kernel(
    place, xo, xb, xh, *refs,
):
    *pieces, gains, qkv0, qkv1, inverse, low_t, up0, up1 = refs[:15]
    x, spread, w, low, up_here, down, rest, sems = refs[15:]
    core, outer, inner = place[0], place[1], place[2]
    wide = 2 * TILE
    tiles = [slice(m * TILE, (m + 1) * TILE) for m in range(3)]
    bands = [slice(n * wide, (n + 1) * wide) for n in range(3)]
    copies = [
        pltpu.make_async_copy(tile, x.at[rows, :], sems.at[m])
        for m, (tile, rows) in enumerate(zip((xo, xb, xh), tiles))
    ]
    for (distance, first), piece in zip(PIECES, pieces):
        i = lax.rem(outer + distance, 4)
        for k in range(piece.shape[0]):
            j = lax.rem(inner + first + k, 4)
            slot = jnp.where(core == 0, 4 * i + j, 4 * j + i)
            sem = sems.at[len(copies)]
            copies.append(pltpu.make_async_copy(piece.at[k], spread.at[slot], sem))
    for copy in copies:
        copy.start()
    inverse[...] = jnp.zeros_like(inverse)
    for copy in copies:
        copy.wait()
    for i in range(16):
        rest[16 * i : 16 * (i + 1), :] = spread[i, 2 * COLS :, :]
    to = lax.broadcasted_iota(jnp.int32, (64, 256), 0)
    source = 16 * (to % 16) + 4 * (to // 16)
    at_column = lax.broadcasted_iota(jnp.int32, (64, 256), 1)

    def adapter_rows(r):
        return dot(jnp.where(at_column == source + r, 1.0, 0.0).astype(BF16), rest[...])

    flat = adapter_rows(0)
    for i in range(24):
        part = flat[:, RANK * i : RANK * (i + 1)]
        down[pl.ds(i, 64, stride=24), :] = jnp.concatenate([part, part], axis=1)
    down_here = down[:, :RANK].astype(BF16)
    up = [adapter_rows(1 + kind).astype(BF16) for kind in range(3)]
    for m, rows in enumerate(tiles):
        part = dot(x[rows, :], down_here)
        low[rows, :] = part.astype(BF16)
        low_t[:, rows] = part.T.astype(BF16)
    kinds = [jnp.where(core == 0, KINDS[0][b], KINDS[1][b]) for b in range(6)]
    for b, kind in enumerate(kinds):
        mine = jnp.zeros((RANK, TILE), BF16)
        for c in range(2):
            at = (2 * c + b // 3) * TILE
            mine = jnp.where(core == c, up[KINDS[c][b]][:, at : at + TILE], mine)
        up_here[:, b * TILE : (b + 1) * TILE] = mine
        (up0, up1)[b // 3][:, pl.ds(pl.multiple_of(kind * TILE, TILE), TILE)] = mine
    for n in range(3):
        for g in range(2 if n == 0 else 0):
            for i in range(16):
                to = (16 * g + i) * COLS
                w[to : to + COLS, :] = spread[i, g * COLS : (g + 1) * COLS, :]
        for rows in tiles:
            raw = rows_dot(x[rows, :], w[bands[n], :]) + dot(low[rows, :], up_here[:, bands[n]])
            for b in (2 * n, 2 * n + 1):
                kind, qkv = kinds[b], (qkv0, qkv1)[b // 3]
                plain = kind == 2
                gain = jnp.where(kind == 0, gains[0:1, :], jnp.where(plain, 1.0, gains[1:2, :]))
                for i in range(GROUP):
                    at = (b - 2 * n) * TILE + i * DIM
                    part = raw[:, at : at + DIM]
                    inv = lax.rsqrt(jnp.mean(part * part, axis=-1, keepdims=True) + EPSILON)
                    inverse[rows, b * GROUP + i : b * GROUP + i + 1] = inv
                    value = part * (jnp.where(plain, 1.0, inv) * gain)
                    to = pl.multiple_of(kind * TILE + i * DIM, DIM)
                    qkv[rows, pl.ds(to, DIM)] = value.astype(BF16)


def project(place, xo, xb, xh, pieces, gains):
    tokens = 3 * TILE
    whole = pl.BlockSpec(memory_space=pltpu.VMEM)
    far = pl.BlockSpec(memory_space=pl.ANY)
    return pl.pallas_call(
        project_kernel,
        in_specs=[SMEM] + [far] * 11 + [whole],
        out_specs=[whole] * 6,
        scratch_shapes=[
            pltpu.VMEM((tokens, FEATURES), BF16),
            pltpu.VMEM((16, ROWS, FEATURES), BF16),
            pltpu.VMEM((6 * TILE, FEATURES), BF16),
            pltpu.VMEM((tokens, RANK), BF16),
            pltpu.VMEM((RANK, 6 * TILE), BF16),
            pltpu.VMEM((FEATURES, DIM), F32),
            pltpu.VMEM((256, FEATURES), BF16),
            pltpu.SemaphoreType.DMA((19,)),
        ],
        out_shape=[shaped(tokens, 3 * TILE)] * 2
        + [shaped(tokens, DIM, dtype=F32), shaped(RANK, tokens)]
        + [shaped(RANK, 3 * TILE)] * 2,
        compiler_params=pltpu.CompilerParams(vmem_limit_bytes=56 << 20),
        cost_estimate=CHEAP,
        name="project",
    )(place, xo, xb, xh, *pieces, gains)


def column_of(inverse, at, rows):
    lane = lax.broadcasted_iota(jnp.int32, (rows, DIM), 1)
    return jnp.sum(jnp.where(lane == at, inverse, 0.0), axis=-1, keepdims=True)


def norm_grad(grad, rounded, gain, inv):
    held = rounded.astype(F32)
    along = jnp.mean(held * grad, axis=-1, keepdims=True)
    return inv * (gain * grad - (held / gain) * along)


def exps_of(key, query):
    return jnp.exp2(rows_dot(key, query) * (SCALE * LOG2E))


def attend_kernel(wide, q, k, v, cot, inverse, gains, out, stats, grad_q, grad_k, grad_v):
    h = pl.program_id(0)
    own = 2 * TILE

    def finish_rows(rows, out_t, delta, inv_sum, grad_t):
        out[rows, :] = out_t.T.astype(BF16)
        inv = column_of(inverse[rows, :], wide[GROUP] + h, rows.stop - rows.start)
        grad_q[rows, :] = norm_grad(grad_t.T, q[rows, :], gains[0:1, :], inv).astype(BF16)

    @pl.when(wide[h] > 0)
    def _():
        key_t = k[...].astype(F32).T.astype(BF16)
        value_t = v[...].astype(F32).T.astype(BF16)
        query, cot_in = q[...], cot[...]
        cot_t = cot_in.astype(F32).T
        exps = exps_of(k[:own, :], query)
        exps_far = exps_of(k[own:, :], query[TILE:])
        total = jnp.sum(exps, axis=0, keepdims=True)
        total_far = jnp.sum(exps_far, axis=0, keepdims=True)
        total = total + jnp.concatenate([jnp.zeros_like(total_far), total_far], axis=1)
        inv_sum = 1.0 / total
        probs, probs_far = exps * inv_sum, exps_far * inv_sum[:, TILE:]
        rounded, rounded_far = probs.astype(BF16), probs_far.astype(BF16)
        out_t = dot(value_t[:, :own], rounded)
        out_far = dot(value_t[:, own:], rounded_far)
        out_t = out_t + jnp.concatenate([jnp.zeros_like(out_far), out_far], axis=1)
        out_t = out_t.astype(BF16).astype(F32)
        delta = jnp.sum(cot_t * out_t, axis=0, keepdims=True)
        scores = (probs * (rows_dot(v[:own, :], cot_in) - delta)).astype(BF16)
        scores_far = (probs_far * (rows_dot(v[own:, :], cot_in[TILE:]) - delta[:, TILE:])).astype(BF16)
        grad_t = dot(key_t[:, :own], scores)
        grad_far = dot(key_t[:, own:], scores_far)
        grad_t = (grad_t + jnp.concatenate([jnp.zeros_like(grad_far), grad_far], axis=1)) * SCALE
        grad_k[...] = dot(scores, query) * SCALE
        grad_v[...] = dot(rounded, cot_in)
        stats[0, 0:1, :] = inv_sum[:, TILE:]
        stats[0, 1:2, :] = delta[:, TILE:]
        finish_rows(slice(0, own), out_t, delta, inv_sum, grad_t)

    @pl.when(wide[h] == 0)
    def _():
        stats[...] = jnp.zeros_like(stats)
        for tile in range(2):
            rows = slice(tile * TILE, (tile + 1) * TILE)
            query, key, value, cot_in = q[rows, :], k[rows, :], v[rows, :], cot[rows, :]
            exps = exps_of(key, query)
            inv_sum = 1.0 / jnp.sum(exps, axis=0, keepdims=True)
            probs = exps * inv_sum
            rounded = probs.astype(BF16)
            out_t = dot(value.astype(F32).T.astype(BF16), rounded).astype(BF16).astype(F32)
            delta = jnp.sum(cot_in.astype(F32).T * out_t, axis=0, keepdims=True)
            scores = (probs * (rows_dot(value, cot_in) - delta)).astype(BF16)
            grad_t = dot(key.astype(F32).T.astype(BF16), scores) * SCALE
            grad_k[rows, :] = dot(scores, query) * SCALE
            grad_v[rows, :] = dot(rounded, cot_in)
            finish_rows(rows, out_t, delta, inv_sum, grad_t)


def finish_kernel(
    wide, q, k, v, cot, stats, inverse, gains, part_k, part_v, grad_q,
    low_t, up_q, up_k, up_v, *refs,
):
    *before, sums, result, sum_k, sum_v, rank_t = refs
    h = pl.program_id(0)

    @pl.when(h == 0)
    def _():
        rank_t[...] = before[0][...] if before else jnp.zeros_like(rank_t)

    sum_k[...] = part_k[...]
    sum_v[...] = part_v[...]

    @pl.when(wide[h] > 0)
    def _():
        query, cot_in = q[...], cot[...]
        key, value = k[TILE:, :], v[TILE:, :]
        probs = exps_of(key, query) * stats[0, 0:1, :]
        scores = (probs * (rows_dot(value, cot_in) - stats[0, 1:2, :])).astype(BF16)
        sum_k[TILE:, :] += dot(scores, query) * SCALE
        sum_v[TILE:, :] += dot(probs.astype(BF16), cot_in)

    inv = column_of(inverse[...], wide[GROUP + 1] + h, 2 * TILE)
    grad_k = norm_grad(sum_k[...], k[...], gains[1:2, :], inv).astype(BF16)
    grad_v = sum_v[...].astype(BF16)
    left = low_t[...]
    for kind, grad in enumerate((grad_q[...], grad_k, grad_v)):
        at = pl.multiple_of(kind * TILE + h * DIM, DIM)
        sums[:, pl.ds(at, DIM)] = dot(left, grad).astype(BF16)
    rank_t[...] += (
        rows_dot(up_q[...], grad_q[...]) + rows_dot(up_k[...], grad_k) + rows_dot(up_v[...], grad_v)
    )

    @pl.when(h == GROUP - 1)
    def _():
        if before:
            _, xo, xb = before
            outer = rank_t[:, :TILE].astype(BF16)
            inner = rank_t[:, TILE:].astype(BF16)
            result[...] = (dot(outer, xo[...]) + dot(inner, xb[...])).astype(BF16)
        else:
            result[...] = rank_t[...]


SMEM = pl.BlockSpec(memory_space=pltpu.SMEM)
CHEAP = pl.CostEstimate(flops=1 << 20, bytes_accessed=1 << 16, transcendentals=0)
PARAMS = pltpu.CompilerParams(vmem_limit_bytes=56 << 20)


def per_head(rows, at=0, block=0):
    return pl.BlockSpec((rows, DIM), lambda h: (block, at + h))


def constant(*shape):
    return pl.BlockSpec(shape, lambda h: (0,) * len(shape))


def shaped(*shape, dtype=BF16):
    return jax.ShapeDtypeStruct(shape, dtype)


def attend(wide, qkv, cot, inverse, gains):
    own = 2 * TILE
    return pl.pallas_call(
        attend_kernel,
        grid=(GROUP,),
        in_specs=[
            SMEM,
            per_head(own),
            per_head(3 * TILE, GROUP),
            per_head(3 * TILE, 2 * GROUP),
            per_head(own),
            constant(own, DIM),
            constant(2, DIM),
        ],
        out_specs=[
            per_head(own),
            pl.BlockSpec((1, 2, TILE), lambda h: (h, 0, 0)),
            per_head(own),
            per_head(own),
            per_head(own),
        ],
        out_shape=[
            shaped(own, GROUP * DIM),
            shaped(GROUP, 2, TILE, dtype=F32),
            shaped(own, GROUP * DIM),
            shaped(own, GROUP * DIM, dtype=F32),
            shaped(own, GROUP * DIM, dtype=F32),
        ],
        compiler_params=PARAMS,
        cost_estimate=CHEAP,
        name="attend",
    )(wide, qkv, qkv, qkv, cot, inverse, gains)


def finish(wide, qkv, cot, stats, inverse, gains, part_k, part_v, grad_q, low_t, up, *before):
    own = 2 * TILE
    result = (
        shaped(RANK, FEATURES) if before else shaped(RANK, own, dtype=F32)
    )
    return pl.pallas_call(
        finish_kernel,
        grid=(GROUP,),
        in_specs=[
            SMEM,
            per_head(TILE, 0, 2),
            per_head(own, GROUP),
            per_head(own, 2 * GROUP),
            per_head(TILE),
            pl.BlockSpec((1, 2, TILE), lambda h: (h, 0, 0)),
            constant(own, DIM),
            constant(2, DIM),
            per_head(own),
            per_head(own),
            per_head(own),
            constant(RANK, own),
            per_head(RANK),
            per_head(RANK, GROUP),
            per_head(RANK, 2 * GROUP),
        ]
        + [constant(*array.shape) for array in before],
        out_specs=[constant(RANK, 3 * TILE), constant(*result.shape)],
        out_shape=[
            shaped(RANK, 3 * TILE),
            result,
        ],
        scratch_shapes=[
            pltpu.VMEM((own, DIM), F32),
            pltpu.VMEM((own, DIM), F32),
            pltpu.VMEM((RANK, own), F32),
        ],
        compiler_params=PARAMS,
        cost_estimate=CHEAP,
        name="finish",
    )(
        wide, qkv, qkv, qkv, cot, stats, inverse, gains, part_k, part_v, grad_q,
        low_t, up, up, up, *before,
    )


def swap(block, axis):
    return lax.ppermute(block, axis, [(0, 1), (1, 0)])


def hop(block, axis, count, step):
    return lax.ppermute(block, axis, [(i, (i + step) % count) for i in range(count)])


def from_above(block, stage, distance):
    pairs = []
    for core in range(2):
        for i in range(4):
            for j in range(4):
                above = (j + distance) % 4
                if core == stage:
                    pairs.append((16 * core + 4 * i + above, 16 * core + 4 * i + j))
                else:
                    pairs.append((16 * core + 4 * above + i, 16 * core + 4 * j + i))
    return lax.ppermute(block, ("c", "y", "x"), pairs)


def pick(options, at):
    out = options[0]
    for i in range(1, len(options)):
        out = jnp.where(at == i, options[i], out)
    return out


def along_z(block, stride):
    pairs = []
    for source in range(8):
        target = (source + stride) % 8
        pairs.append((ring_index(source, 0), ring_index(target, 0)))
        pairs.append((ring_index(target, 1), ring_index(source, 1)))
    return lax.ppermute(block, ("zh", "c", "zl"), pairs)


def ring_index(z, core):
    return (z // 4) * 8 + core * 4 + z % 4


def gather_first(packed, ready):
    core, zl = lax.axis_index("c"), lax.axis_index("zl")
    spot = lax.axis_index("y") * 4 + lax.axis_index("x")
    along = ("zh", "zl")
    planes = [packed, hop(packed, along, 8, -1), hop(packed, along, 8, 2), hop(packed, along, 8, 1)]
    planes, ready = lax.optimization_barrier((planes, ready))
    third = (spot * COLS + lax.broadcasted_iota(jnp.int32, (COLS, 1), 0)) // TILE
    first = jnp.where(core == 0, pick([0, 1, 2], third), pick([2, 3, 0], third))
    second = jnp.where(core == 0, pick([3, 0, 1], third), pick([1, 2, 3], third))
    columns, small = [plane[:COLS] for plane in planes], [plane[COLS:] for plane in planes]
    block = jnp.concatenate(
        [pick(columns, lax.rem(group - zl + 4, 4)) for group in (first, second)]
        + [pick(small, lax.rem(plane - zl + 4, 4)) for plane in range(4)]
    )
    return block, ready


def gather_second(low, high, crossing):
    above_low, below_high = from_above(low, 1, 1), from_above(high, 1, 3)
    above_high, below_low = from_above(high, 1, 1), from_above(low, 1, 3)
    far = [from_above(above_low, 1, 1), from_above(below_high, 1, 3)]
    near = [above_low, above_high, below_low, below_high]
    crossing = lax.optimization_barrier((crossing, *near))[0]
    return [low, high, *near, *far], crossing


def reduce_adapter(first, second, out_down):
    core = lax.axis_index("c")
    width = GROUP * DIM
    down = out_down.reshape(RANK, 64, FEATURES // 64).transpose(1, 2, 0).reshape(64, FEATURES)
    payload = jnp.concatenate([first, second, down], axis=1)
    parts = lax.all_to_all(payload, FSDP, 0, 0, tiled=True)
    mine = jnp.sum(parts.astype(F32), axis=0).reshape(-1, DIM)
    every = lax.all_gather(mine, ("zh", "c")).reshape(2, 2, -1)
    both = every[0] + every[1]
    grad_up = jnp.concatenate(
        [
            both[side, (3 * group + kind) * width : (3 * group + kind + 1) * width]
            for kind in range(3)
            for side in range(2)
            for group in range(2)
        ]
    )
    grad_down = (both[0] + both[1])[6 * width :]
    return grad_down.reshape(FEATURES // 64, RANK), grad_up.reshape(1, -1)


def local(hidden, modulation, cotangent, frozen, down, up, gains, windows):
    high, core = lax.axis_index("zh"), lax.axis_index("c")
    outermost = core == high
    packed = jnp.concatenate([frozen.T, down.reshape(1, FEATURES), up.reshape(3, FEATURES)])
    packed, hidden = lax.optimization_barrier((packed, hidden))
    own = modulated_norm(hidden[0], modulation[0])
    other = swap(own, "c")
    width = HALF * DIM
    xo = jnp.where(outermost, own, other)
    xb = jnp.where(outermost, other, own)
    half = lax.dynamic_slice(xb, (core * (TILE // 2), 0), (TILE // 2, FEATURES))
    cot_own = lax.dynamic_slice(cotangent[0], (0, core * width), (TILE, width))
    cot_other = swap(lax.dynamic_slice(cotangent[0], (0, (1 - core) * width), (TILE, width)), "c")
    block, (half, cot_other) = gather_first(packed, (half, cot_other))
    ring = [block] + [from_above(block, 0, distance) for distance in (1, 2, 3)]
    ring, near = lax.optimization_barrier((ring, along_z(half, 1)))
    pieces, near = gather_second(jnp.stack(ring[:2]), jnp.stack(ring[2:]), along_z(near, 3))
    far = swap(near, "c")
    xh = jnp.concatenate([jnp.where(core == 0, near, far), jnp.where(core == 0, far, near)])
    cot_edge = jnp.where(outermost, cot_other, cot_own)
    cot = jnp.concatenate([jnp.where(outermost, cot_own, cot_other), cot_edge])

    wide = (lax.dynamic_slice(windows, (core * HALF,), (HALF,)) > 1).astype(jnp.int32)
    xh, cot_edge = lax.optimization_barrier((xh, cot_edge))
    cot_halo = swap(cot_edge, "zh")
    y, x = lax.axis_index("y"), lax.axis_index("x")
    place = jnp.stack([core, jnp.where(core == 0, y, x), jnp.where(core == 0, x, y)])
    qkv0, qkv1, inverse, low_t, up0, up1 = project(place, xo, xb, xh, pieces, gains)
    groups = (qkv0, up0), (qkv1, up1)

    heads = []
    for g in range(2):
        lanes = [
            GROUP * jnp.where(core == 0, *(KINDS[c].index(kind, 3 * g, 3 * g + 3) for c in (0, 1)))
            for kind in (0, 1)
        ]
        heads.append(jnp.stack([*wide[GROUP * g : GROUP * (g + 1)], *lanes]).astype(jnp.int32))
    back, kept, sums = [], [], []
    held, exchanged = [], []
    for g, (qkv, _) in enumerate(groups):
        cot_g = cot[:, g * GROUP * DIM : (g + 1) * GROUP * DIM]
        out, stats, grad_q, part_k, part_v = attend(heads[g], qkv, cot_g, inverse, gains)
        tiles = out[:TILE], out[TILE:]
        back.append(swap(jnp.where(outermost, tiles[1], tiles[0]), "c"))
        kept.append(jnp.where(outermost, tiles[0], tiles[1]))
        held.append((*groups[g], stats, part_k, part_v, grad_q))
        exchanged.append(swap(stats, "zh"))
    held = lax.optimization_barrier(held)
    for g, (qkv, up_mine, _, part_k, part_v, grad_q) in enumerate(held):
        part, result = finish(
            heads[g], qkv, cot_halo[:, g * GROUP * DIM : (g + 1) * GROUP * DIM], exchanged[g], inverse, gains, part_k, part_v, grad_q, low_t, up_mine, *([result, xo, xb] if g else []),
        )
        sums.append(part)
    sides = [jnp.where(core == side, kept[g], back[g]) for side in range(2) for g in range(2)]
    attn_out = jnp.concatenate(sides, axis=1)
    grad_down, grad_up = reduce_adapter(sums[0], sums[1], result)
    return attn_out[None], grad_down, grad_up


def solution(mesh):
    split = Mesh(mesh.devices.reshape(2, 2, 4, 4, 4), AXES)
    sp = ("zh", "c")
    in_specs = (
        P(FSDP, sp, None),
        P(FSDP, None, None),
        P(FSDP, sp, None),
        P(None, FSDP),
        P(FSDP, None),
        P(FSDP, None),
        P(),
        P(),
    )
    out_specs = (P(FSDP, sp, None), P(FSDP, None), P(FSDP, None))
    return jax.shard_map(local, mesh=split, in_specs=in_specs, out_specs=out_specs, check_vma=False)
```
